256 devices in a mesh: dp: 2 (over core), row: 16 (over x, y), col: 8 (over z).
Axes of the slice: x: 4, y: 4, z: 8, core: 2. Of those that a mesh axis runs over, the one named last changes fastest.
Arguments:
- tokens: bfloat16 [2048, 8192], P(('dp', 'col'), 'row'), may hold values from -6 to 6
- cotangent: bfloat16 [2048, 8192], P(('dp', 'col'), 'row'), may hold values from -6 to 6
- gate_weight: bfloat16 [8192, 14336], P('row', 'col'), may hold values from -0.0625 to 0.0625
- up_weight: bfloat16 [8192, 14336], P('row', 'col'), may hold values from -0.0625 to 0.0625
- down_weight: bfloat16 [14336, 8192], P('col', 'row'), may hold values from -0.046875 to 0.046875
Outputs:
- mixed: bfloat16 [2048, 8192], P(('dp', 'col'), 'row')
- input_grad: bfloat16 [2048, 8192], P(('dp', 'col'), 'row')
- gate_grad: bfloat16 [8192, 14336], P('row', 'col')
- up_grad: bfloat16 [8192, 14336], P('row', 'col')
- down_grad: bfloat16 [14336, 8192], P('col', 'row')
The draws below stay inside these ranges and needn't reach their ends.
All inputs are finite; a program needn't handle non-finite values.
Results may differ from the reference program's by a relative error of at most 0.0059.
Values may be sent and summed in bfloat16 or wider, within the bound.
No kernel may reach another device: no remote copies, remote signals or barrier semaphores. Data moves between devices by JAX's collectives and lax.ppermute only.
A program may use at most 128 MiB of HBM per device.

```python
import jax
import jax.numpy as jnp
from jax import lax

D = 8192
FF = 14336
TOK_DEV = 1024
TOKENS = 2048
N_DP = 2


def level_of(stream_key, extent, split, low, high):
    def one(dim, parts):
        steps = jax.random.uniform(jax.random.fold_in(jax.random.fold_in(stream_key, 6), dim), (parts,), jnp.float32, low / len(split), high / len(split))
        return jnp.repeat(jnp.exp(steps), extent[dim] // parts).reshape((-1,) + (1,) * (len(extent) - dim - 1))

    loudness = one(*split[0])
    for cut in split[1:]:
        loudness = loudness * one(*cut)
    return loudness


def centred(stream_key, dims, deviation, reach, cuts=(), dtype=jnp.bfloat16):
    drawn = deviation * jax.random.normal(stream_key, dims, jnp.float32)
    if cuts:
        drawn = drawn * level_of(stream_key, dims, cuts, -0.22, 0.18)
    return jnp.clip(drawn, -reach, reach).astype(dtype)


def setup_inputs(seed: int = 0) -> dict:
    streams_of = jax.random.split(jax.random.key(seed), 6)
    tokens = centred(streams_of[0], (TOKENS, D), 1.0, 6.0, ((0, 16), (1, 16)))
    cotangent = centred(streams_of[1], (TOKENS, D), 1.0, 6.0, ((0, 16), (1, 16)))
    gate_weight = centred(streams_of[2], (D, FF), D ** -0.5, 0.0625, ((0, 16), (1, 8)))
    up_weight = centred(streams_of[3], (D, FF), D ** -0.5, 0.0625, ((0, 16), (1, 8)))
    down_weight = centred(streams_of[4], (FF, D), FF ** -0.5, 0.046875, ((0, 8), (1, 16)))
    return {"tokens": tokens, "cotangent": cotangent, "gate_weight": gate_weight, "up_weight": up_weight, "down_weight": down_weight}


def contract_rows(left, right):
    return lax.dot_general(left, right, (((0,), (0,)), ((), ())), preferred_element_type=jnp.float32)


def contract_cols(left, right):
    return lax.dot_general(left, right, (((1,), (1,)), ((), ())), preferred_element_type=jnp.float32)


def rounded(value):
    return lax.optimization_barrier(value.astype(jnp.bfloat16)).astype(jnp.float32)


def reference(tokens, cotangent, gate_weight, up_weight, down_weight):
    mixed_rows = []
    input_rows = []
    gate_total = jnp.zeros(gate_weight.shape, jnp.float32)
    up_total = jnp.zeros(up_weight.shape, jnp.float32)
    down_total = jnp.zeros(down_weight.shape, jnp.float32)
    for replica in range(N_DP):
        inputs = tokens[replica * TOK_DEV:(replica + 1) * TOK_DEV]
        upstream = cotangent[replica * TOK_DEV:(replica + 1) * TOK_DEV]
        gate = jnp.dot(inputs, gate_weight, preferred_element_type=jnp.float32)
        up_val = jnp.dot(inputs, up_weight, preferred_element_type=jnp.float32)
        sigma = jax.nn.sigmoid(gate)
        hidden = (gate * sigma * up_val).astype(jnp.bfloat16)
        mixed_rows.append(jnp.dot(hidden, down_weight, preferred_element_type=jnp.float32).astype(jnp.bfloat16))
        dhidden = contract_cols(upstream, down_weight)
        dgate = (dhidden * up_val * sigma * (1.0 + gate * (1.0 - sigma))).astype(jnp.bfloat16)
        dup_val = (dhidden * gate * sigma).astype(jnp.bfloat16)
        dinput = contract_cols(dgate, gate_weight) + contract_cols(dup_val, up_weight)
        input_rows.append(dinput.astype(jnp.bfloat16))
        gate_total = gate_total + rounded(contract_rows(inputs, dgate))
        up_total = up_total + rounded(contract_rows(inputs, dup_val))
        down_total = down_total + rounded(contract_rows(hidden, upstream))
    mixed = jnp.concatenate(mixed_rows, axis=0)
    input_grad = jnp.concatenate(input_rows, axis=0)
    return (mixed, input_grad, gate_total.astype(jnp.bfloat16), up_total.astype(jnp.bfloat16), down_total.astype(jnp.bfloat16))
```

```python
import functools

import jax
import jax.numpy as jnp
from jax import lax
from jax.experimental import pallas as pl
from jax.experimental.pallas import tpu as pltpu
from jax.sharding import PartitionSpec as P

F32 = jnp.float32
BF16 = jnp.bfloat16

ROW_PAIRS = (
    [(i, (i // 4) * 4 + ((i % 4) ^ 1)) for i in range(16)],
    [(i, (i // 4) * 4 + (3 - i % 4)) for i in range(16)],
    [(i, ((i // 4) ^ 1) * 4 + i % 4) for i in range(16)],
    [(i, (3 - i // 4) * 4 + i % 4) for i in range(16)],
)

STREAMS = (
    ((1, -1), (0, 2, 1, 3)),
    ((2, -2), (2, 0, 3, 1)),
    ((3, -3), (1, 3, 0, 2)),
    ((0, 4), (3, 1, 2, 0)),
)

BLOCK = 128
TILE = 256


def exchange(value, pairs):
    return lax.ppermute(value, "row", ROW_PAIRS[pairs])


def along_col(value, distance):
    return lax.ppermute(value, "col", [(i, (i - distance) % 8) for i in range(8)])


def label_bits():
    index = lax.axis_index("row")
    x, y = index // 4, index % 4
    return ((y >> 1) ^ (y & 1), y >> 1, (x >> 1) ^ (x & 1), x >> 1)


def order_matrix(flip, blocks, which, inverse):
    rows = BLOCK * blocks
    shape = (BLOCK, rows) if inverse else (rows, BLOCK)
    local = lax.broadcasted_iota(jnp.int32, shape, 1 if inverse else 0)
    plain = lax.broadcasted_iota(jnp.int32, shape, 0 if inverse else 1)
    shift = 4 + (blocks - 1)
    wanted = (((local >> shift) ^ flip) << 4) + (local & 15)
    hit = (wanted == plain) & (((local >> 4) & (blocks - 1)) == which)
    return jnp.where(hit, 1.0, 0.0).astype(BF16)


def dot_cols(left, right):
    return lax.dot_general(left, right, (((1,), (1,)), ((), ())), preferred_element_type=F32)


def dot_rows(left, right):
    return lax.dot_general(left, right, (((0,), (0,)), ((), ())), preferred_element_type=F32)


def terms_kernel(blocks, flip_ref, *refs):
    both = refs[:blocks]
    gate_w, up_w, down_w, rows_ref, send_ref, keep_ref = refs[blocks:]
    width = gate_w.shape[0]
    half = BLOCK * blocks // 2

    @pl.when(pl.program_id(0) == 0)
    def _():
        total = None
        for which in range(blocks):
            part = jnp.dot(
                order_matrix(flip_ref[0], blocks, which, False), both[which][...], preferred_element_type=F32
            )
            total = part if total is None else total + part
        rows_ref[...] = total.astype(BF16)

    inputs = rows_ref[:, :width]
    upstream = rows_ref[:, width:]
    for index, value in enumerate(
        (
            jnp.dot(inputs, gate_w[...], preferred_element_type=F32),
            jnp.dot(inputs, up_w[...], preferred_element_type=F32),
            dot_cols(upstream, down_w[...]),
        )
    ):
        keep_ref[index] = value[:half]
        send_ref[index] = value[half:].astype(BF16)


def terms(blocks, flip, both, gate_w, up_w, down_w):
    width, hidden = gate_w.shape
    rows = BLOCK * blocks
    return pl.pallas_call(
        functools.partial(terms_kernel, blocks),
        grid=(hidden // TILE,),
        in_specs=[pl.BlockSpec(memory_space=pltpu.SMEM)]
        + [pl.BlockSpec((BLOCK, 2 * width), lambda i: (0, 0))] * blocks
        + [
            pl.BlockSpec((width, TILE), lambda i: (0, i)),
            pl.BlockSpec((width, TILE), lambda i: (0, i)),
            pl.BlockSpec((TILE, width), lambda i: (i, 0)),
        ],
        out_specs=[
            pl.BlockSpec((rows, 2 * width), lambda i: (0, 0)),
            pl.BlockSpec((3, rows // 2, TILE), lambda i: (0, 0, i)),
            pl.BlockSpec((3, rows // 2, TILE), lambda i: (0, 0, i)),
        ],
        out_shape=[
            jax.ShapeDtypeStruct((rows, 2 * width), BF16),
            jax.ShapeDtypeStruct((3, rows // 2, hidden), BF16),
            jax.ShapeDtypeStruct((3, rows // 2, hidden), F32),
        ],
        compiler_params=pltpu.CompilerParams(vmem_limit_bytes=24 << 20),
        cost_estimate=pl.CostEstimate(
            flops=6 * rows * width * hidden, bytes_accessed=6 * width * hidden + 9 * rows * hidden, transcendentals=0
        ),
    )(flip, *both, gate_w, up_w, down_w)


def add_rows_kernel(keep_ref, got_ref, send_ref, next_ref):
    half = send_ref.shape[1]
    total = keep_ref[...] + got_ref[...].astype(F32)
    next_ref[...] = total[:, :half]
    send_ref[...] = total[:, half:].astype(BF16)


def add_rows(keep, got):
    three, rows, hidden = keep.shape
    whole = pl.BlockSpec((1, rows, hidden), lambda i: (i, 0, 0))
    half = pl.BlockSpec((1, rows // 2, hidden), lambda i: (i, 0, 0))
    return pl.pallas_call(
        add_rows_kernel,
        grid=(three,),
        in_specs=[whole, whole],
        out_specs=[half, half],
        out_shape=[
            jax.ShapeDtypeStruct((three, rows // 2, hidden), BF16),
            jax.ShapeDtypeStruct((three, rows // 2, hidden), F32),
        ],
        compiler_params=pltpu.CompilerParams(vmem_limit_bytes=24 << 20),
        cost_estimate=pl.CostEstimate(flops=keep.size, bytes_accessed=9 * keep.size, transcendentals=0),
    )(keep, got)


def add_cols_kernel(bit_ref, keep_ref, got_ref, send_ref, next_ref):
    half = send_ref.shape[2]
    total = keep_ref[...] + got_ref[...].astype(F32)
    low, high = total[:, :, :half], total[:, :, half:]
    upper = bit_ref[0] == 1
    next_ref[...] = jnp.where(upper, high, low)
    send_ref[...] = jnp.where(upper, low, high).astype(BF16)


def add_cols(bit, keep, got):
    three, rows, hidden = keep.shape
    return pl.pallas_call(
        add_cols_kernel,
        in_specs=[pl.BlockSpec(memory_space=pltpu.SMEM)] + [pl.BlockSpec(memory_space=pltpu.VMEM)] * 2,
        out_specs=[pl.BlockSpec(memory_space=pltpu.VMEM)] * 2,
        out_shape=[
            jax.ShapeDtypeStruct((three, rows, hidden // 2), BF16),
            jax.ShapeDtypeStruct((three, rows, hidden // 2), F32),
        ],
        compiler_params=pltpu.CompilerParams(vmem_limit_bytes=24 << 20),
        cost_estimate=pl.CostEstimate(flops=keep.size, bytes_accessed=9 * keep.size, transcendentals=0),
    )(bit, keep, got)


def activate_kernel(keep_ref, got_ref, out_ref):
    gate = keep_ref[0] + got_ref[0].astype(F32)
    up_val = keep_ref[1] + got_ref[1].astype(F32)
    dhidden = keep_ref[2] + got_ref[2].astype(F32)
    sigma = jax.nn.sigmoid(gate)
    out_ref[0] = (gate * sigma * up_val).astype(BF16)
    out_ref[1] = (dhidden * up_val * sigma * (1.0 + gate * (1.0 - sigma))).astype(BF16)
    out_ref[2] = (dhidden * gate * sigma).astype(BF16)


def activate(keep, got):
    return pl.pallas_call(
        activate_kernel,
        in_specs=[pl.BlockSpec(memory_space=pltpu.VMEM)] * 2,
        out_specs=pl.BlockSpec(memory_space=pltpu.VMEM),
        out_shape=jax.ShapeDtypeStruct(keep.shape, BF16),
        compiler_params=pltpu.CompilerParams(vmem_limit_bytes=24 << 20),
        cost_estimate=pl.CostEstimate(flops=4 * keep.size, bytes_accessed=8 * keep.size, transcendentals=keep.size),
    )(keep, got)


def results_kernel(blocks, flip_ref, near_ref, far_ref, gate_w, up_w, down_w, *refs):
    outs, (mixed_sum, input_sum) = refs[:blocks], refs[blocks:]
    width = gate_w.shape[0]
    step = pl.program_id(0)

    @pl.when(step == 0)
    def _():
        mixed_sum[...] = jnp.zeros_like(mixed_sum)
        input_sum[...] = jnp.zeros_like(input_sum)

    def tall(index):
        return jnp.concatenate([near_ref[index], far_ref[index]], axis=0)

    mixed_sum[...] += jnp.dot(tall(0), down_w[...], preferred_element_type=F32)
    input_sum[...] += dot_cols(tall(1), gate_w[...]) + dot_cols(tall(2), up_w[...])

    @pl.when(step == pl.num_programs(0) - 1)
    def _():
        mixed = mixed_sum[...].astype(BF16)
        input_grad = input_sum[...].astype(BF16)
        for which in range(blocks):
            back = order_matrix(flip_ref[0], blocks, which, True)
            outs[which][:, :width] = jnp.dot(back, mixed, preferred_element_type=F32).astype(BF16)
            outs[which][:, width:] = jnp.dot(back, input_grad, preferred_element_type=F32).astype(BF16)


def results(blocks, flip, near, far, gate_w, up_w, down_w):
    width, hidden = gate_w.shape
    rows = BLOCK * blocks
    part = pl.BlockSpec((3, rows // 2, TILE), lambda i: (0, 0, i))
    return pl.pallas_call(
        functools.partial(results_kernel, blocks),
        grid=(hidden // TILE,),
        in_specs=[
            pl.BlockSpec(memory_space=pltpu.SMEM),
            part,
            part,
            pl.BlockSpec((width, TILE), lambda i: (0, i)),
            pl.BlockSpec((width, TILE), lambda i: (0, i)),
            pl.BlockSpec((TILE, width), lambda i: (i, 0)),
        ],
        out_specs=[pl.BlockSpec((BLOCK, 2 * width), lambda i: (0, 0))] * blocks,
        out_shape=[jax.ShapeDtypeStruct((BLOCK, 2 * width), BF16)] * blocks,
        scratch_shapes=[pltpu.VMEM((rows, width), F32)] * 2,
        compiler_params=pltpu.CompilerParams(vmem_limit_bytes=24 << 20),
        cost_estimate=pl.CostEstimate(
            flops=6 * rows * width * hidden, bytes_accessed=6 * width * hidden + 6 * rows * hidden, transcendentals=0
        ),
    )(flip, near, far, gate_w, up_w, down_w)


def down_kernel(streams, *refs):
    upstream, pieces, out_ref = refs[:streams], refs[streams:-1], refs[-1]
    hidden = jnp.concatenate([piece[0] for piece in pieces], axis=0)
    cotangent = jnp.concatenate([rows[...] for rows in upstream], axis=0)
    out_ref[...] = dot_rows(hidden, cotangent).astype(BF16)


def input_kernel(streams, *refs):
    inputs, pieces, out_ref, turned = refs[:streams], refs[streams:-2], refs[-2], refs[-1]

    @pl.when(pl.program_id(0) == 0)
    def _():
        turned[...] = jnp.concatenate([rows[...] for rows in inputs], axis=0).T

    grads = jnp.concatenate([piece[0] for piece in pieces], axis=0)
    out_ref[...] = jnp.dot(turned[...], grads, preferred_element_type=F32).astype(BF16)


def weight_grad(which, rows, pieces):
    width = rows[0].shape[1] // 2
    hidden = pieces[0].shape[2]
    tokens = sum(r.shape[0] for r in rows)
    side = 1 if which == 0 else 0
    in_specs = [pl.BlockSpec((r.shape[0], width), lambda i: (0, side)) for r in rows]
    in_specs += [pl.BlockSpec((1, p.shape[1], TILE), lambda i: (which, 0, i)) for p in pieces]
    if which == 0:
        kernel, out, block, scratch = down_kernel, (hidden, width), pl.BlockSpec((TILE, width), lambda i: (i, 0)), []
    else:
        kernel, out, block = input_kernel, (width, hidden), pl.BlockSpec((width, TILE), lambda i: (0, i))
        scratch = [pltpu.VMEM((width, tokens), BF16)]
    return pl.pallas_call(
        functools.partial(kernel, len(rows)),
        grid=(hidden // TILE,),
        in_specs=in_specs,
        out_specs=block,
        out_shape=jax.ShapeDtypeStruct(out, BF16),
        scratch_shapes=scratch,
        compiler_params=pltpu.CompilerParams(vmem_limit_bytes=32 << 20),
        cost_estimate=pl.CostEstimate(
            flops=2 * tokens * width * hidden, bytes_accessed=2 * (tokens + width) * hidden, transcendentals=0
        ),
    )(*rows, *pieces)


def on_device(tokens, cotangent, gate_w, up_w, down_w):
    width = tokens.shape[1]
    bits = label_bits()
    blocks_at = {0: jnp.concatenate([tokens, cotangent], axis=1)}
    for distance in (1, 2, 3, 4):
        blocks_at[distance] = along_col(blocks_at[distance - 1], 1)
        if distance < 4:
            blocks_at[-distance] = along_col(blocks_at[1 - distance], -1)

    def one(value):
        return jnp.reshape(value, (1,)).astype(jnp.int32)

    rows, pieces = [], []
    sums = None
    for owners, order in STREAMS:
        count = len(owners)
        flip = one(bits[order[0]] * 4 + bits[order[1]] * 2 + bits[order[2]])
        upper = bits[order[3]]
        local, send, keep = terms(count, flip, [blocks_at[o] for o in owners], gate_w, up_w, down_w)
        send, keep = add_rows(keep, exchange(send, order[0]))
        send, keep = add_rows(keep, exchange(send, order[1]))
        send, keep = add_cols(one(upper), keep, exchange(send, order[2]))
        near = activate(keep, exchange(send, order[3]))
        got = exchange(near, order[3])
        near = jnp.concatenate([jnp.where(upper == 1, got, near), jnp.where(upper == 1, near, got)], axis=2)
        near = jnp.concatenate([near, exchange(near, order[2])], axis=1)
        near = jnp.concatenate([near, exchange(near, order[1])], axis=1)
        far = exchange(near, order[0])
        rows.append(local)
        pieces += [near, far]
        for owner, part in zip(owners, results(count, flip, near, far, gate_w, up_w, down_w)):
            if owner:
                part = along_col(part, -owner)
            part = part.astype(F32)
            sums = part if sums is None else sums + part

    down_term = weight_grad(0, rows, pieces)
    down_other = lax.ppermute(down_term, "dp", [(0, 1), (1, 0)])
    gate_term = weight_grad(1, rows, pieces)
    gate_other = lax.ppermute(gate_term, "dp", [(0, 1), (1, 0)])
    up_term = weight_grad(2, rows, pieces)
    up_other = lax.ppermute(up_term, "dp", [(0, 1), (1, 0)])

    def both(left, right):
        return (left.astype(F32) + right.astype(F32)).astype(BF16)

    return (
        sums[:, :width].astype(BF16),
        sums[:, width:].astype(BF16),
        both(gate_term, gate_other),
        both(up_term, up_other),
        both(down_term, down_other),
    )


def solution(mesh):
    specs = (
        P(("dp", "col"), "row"),
        P(("dp", "col"), "row"),
        P("row", "col"),
        P("row", "col"),
        P("col", "row"),
    )
    return jax.shard_map(on_device, mesh=mesh, in_specs=specs, out_specs=specs, check_vma=False)
```

```python
import jax
import jax.numpy as jnp
from jax import lax
from jax.experimental import pallas as pl
from jax.experimental.pallas import tpu as pltpu
from jax.sharding import PartitionSpec as P

F32 = jnp.float32
BF16 = jnp.bfloat16

ROW_PAIRS = (
    [(i, (i // 4) * 4 + ((i % 4) ^ 1)) for i in range(16)],
    [(i, (i // 4) * 4 + (3 - i % 4)) for i in range(16)],
    [(i, ((i // 4) ^ 1) * 4 + i % 4) for i in range(16)],
    [(i, (3 - i // 4) * 4 + i % 4) for i in range(16)],
)

WHOLE = (0, 1)
HALVED = (
    ((-1, 2), (0, 1), (2, 3)),
    ((-2, 3), (2, 3), (0, 1)),
    ((-3, 4), (1, 0), (3, 2)),
)

ORDER = "W012001102210201122W012W"

BLOCK = 128
TILE = 256
GROUP = 16
VMEM = pl.BlockSpec(memory_space=pltpu.VMEM)
SMEM = pl.BlockSpec(memory_space=pltpu.SMEM)
ANY = pl.BlockSpec(memory_space=pl.ANY)


class Line:
    def __init__(self):
        self.last = None

    def call(self, kernel, args, in_specs, out_specs, out_shape, flops, moved, grid=(), scratch=(), vmem=24, turns=0):
        inputs = len(args)
        skip = 0 if self.last is None else 1

        def body(*refs):
            kernel(*refs[:inputs], *refs[inputs + skip:])

        out = pl.pallas_call(
            body,
            grid=grid,
            in_specs=list(in_specs) + [ANY] * skip,
            out_specs=out_specs,
            out_shape=out_shape,
            scratch_shapes=scratch,
            compiler_params=pltpu.CompilerParams(vmem_limit_bytes=vmem << 20),
            cost_estimate=pl.CostEstimate(flops=1, bytes_accessed=1, transcendentals=0),
        )(*args, *([self.last] if skip else []))
        self.last = out[0] if isinstance(out_shape[0], jax.ShapeDtypeStruct) else far(out[0])
        return out


def far(value):
    return pltpu.with_memory_space_constraint(value, pltpu.HBM)


def hbm(shape, dtype):
    return pltpu.HBM(shape, dtype)


def exchange(value, pairs):
    return lax.ppermute(value, "row", ROW_PAIRS[pairs])


def along_col(value, distance):
    return lax.ppermute(value, "col", [(i, (i - distance) % 8) for i in range(8)])


def label_bits():
    index = lax.axis_index("row")
    x, y = index // 4, index % 4
    return ((y >> 1) ^ (y & 1), y >> 1, (x >> 1) ^ (x & 1), x >> 1)


def order_matrix(flip, inverse):
    local = lax.broadcasted_iota(jnp.int32, (BLOCK, BLOCK), 1 if inverse else 0)
    plain = lax.broadcasted_iota(jnp.int32, (BLOCK, BLOCK), 0 if inverse else 1)
    return jnp.where((local ^ (flip * GROUP)) == plain, 1.0, 0.0).astype(BF16)


def dot(left, right):
    return jnp.dot(left, right, preferred_element_type=F32)


def dot_cols(left, right):
    return lax.dot_general(left, right, (((1,), (1,)), ((), ())), preferred_element_type=F32)


def dot_rows(left, right):
    return lax.dot_general(left, right, (((0,), (0,)), ((), ())), preferred_element_type=F32)


def whole_terms(line, blocks, weights):
    gate_w, up_w, down_w = weights
    width, hidden = gate_w.shape
    tile = hidden // 2
    rows = 2 * BLOCK

    def kernel(first, second, gate_ref, up_ref, down_ref, out_ref):
        part = pl.program_id(0)
        both = jnp.concatenate([first[...], second[...]], axis=0)

        @pl.when(part == 0)
        def _():
            out_ref[...] = dot(both[:, :width], gate_ref[...])

        @pl.when(part == 1)
        def _():
            out_ref[...] = dot(both[:, :width], up_ref[...])

        @pl.when(part == 2)
        def _():
            out_ref[...] = dot_cols(both[:, width:], down_ref[...])

    def at(which):
        return lambda p, i: jnp.where(p < which, 0, jnp.where(p == which, i, 1))

    block = pl.BlockSpec((BLOCK, 2 * width), lambda p, i: (0, 0))
    return line.call(
        kernel,
        [*blocks, *map(far, weights)],
        [
            block,
            block,
            pl.BlockSpec((width, tile), lambda p, i: (0, at(0)(p, i))),
            pl.BlockSpec((width, tile), lambda p, i: (0, at(1)(p, i))),
            pl.BlockSpec((tile, width), lambda p, i: (at(2)(p, i), 0)),
        ],
        [pl.BlockSpec((rows, tile), lambda p, i: (0, 2 * p + i))],
        [hbm((rows, 3 * hidden), F32)],
        flops=6 * rows * width * hidden,
        moved=6 * width * hidden + 12 * rows * hidden,
        grid=(3, 2),
    )[0]


def halved_terms(line, blocks, flips, weights):
    gate_w, up_w, down_w = weights
    width, hidden = gate_w.shape
    half = BLOCK // 2

    def kernel(flip_ref, first, second, gate_ref, up_ref, down_ref, rows_ref, send0, keep0, send1, keep1):
        @pl.when(pl.program_id(0) == 0)
        def _():
            for j, block in enumerate((first, second)):
                rows_ref[j * BLOCK:(j + 1) * BLOCK] = dot(order_matrix(flip_ref[j], False), block[...]).astype(BF16)

        inputs, upstream = rows_ref[:, :width], rows_ref[:, width:]
        values = (dot(inputs, gate_ref[...]), dot(inputs, up_ref[...]), dot_cols(upstream, down_ref[...]))
        for index, value in enumerate(values):
            for j, (send, keep) in enumerate(((send0, keep0), (send1, keep1))):
                keep[index] = value[j * BLOCK:j * BLOCK + half]
                send[index] = value[j * BLOCK + half:(j + 1) * BLOCK].astype(BF16)

    block = pl.BlockSpec((BLOCK, 2 * width), lambda i: (0, 0))
    part = pl.BlockSpec((3, half, TILE), lambda i: (0, 0, i))
    shape = (3, half, hidden)
    return line.call(
        kernel,
        [flips, *blocks, *map(far, weights)],
        [
            SMEM,
            block,
            block,
            pl.BlockSpec((width, TILE), lambda i: (0, i)),
            pl.BlockSpec((width, TILE), lambda i: (0, i)),
            pl.BlockSpec((TILE, width), lambda i: (i, 0)),
        ],
        [pl.BlockSpec((2 * BLOCK, 2 * width), lambda i: (0, 0)), part, part, part, part],
        [hbm((2 * BLOCK, 2 * width), BF16)] + [hbm(shape, BF16), hbm(shape, F32)] * 2,
        flops=12 * BLOCK * width * hidden,
        moved=6 * width * hidden + 18 * BLOCK * hidden,
        grid=(hidden // TILE,),
    )


def add_rows(line, keeps, gots):
    count = len(keeps)
    _, rows, hidden = keeps[0].shape
    half = rows // 2

    def kernel(*refs):
        send, keep = refs[2 * count:]
        for j in range(count):
            total = refs[j][...] + refs[count + j][...].astype(F32)
            keep[:, j * half:(j + 1) * half] = total[:, :half]
            send[:, j * half:(j + 1) * half] = total[:, half:].astype(BF16)

    whole = pl.BlockSpec((1, rows, hidden), lambda i: (i, 0, 0))
    out = pl.BlockSpec((1, count * half, hidden), lambda i: (i, 0, 0))
    shape = (3, count * half, hidden)
    return line.call(
        kernel,
        [*map(far, keeps), *gots],
        [whole] * (2 * count),
        [out, out],
        [hbm(shape, BF16), hbm(shape, F32)],
        flops=3 * count * rows * hidden,
        moved=27 * count * rows * hidden,
        grid=(3,),
    )


def add_cols(line, bit, keep, got):
    _, rows, hidden = keep.shape
    half = hidden // 2

    def kernel(bit_ref, keep_ref, got_ref, send_ref, next_ref):
        total = keep_ref[...] + got_ref[...].astype(F32)
        low, high = total[:, :, :half], total[:, :, half:]
        upper = bit_ref[0] == 1
        next_ref[...] = jnp.where(upper, high, low)
        send_ref[...] = jnp.where(upper, low, high).astype(BF16)

    shape = (3, rows, half)
    return line.call(
        kernel,
        [bit, keep, got],
        [SMEM, VMEM, VMEM],
        [VMEM, VMEM],
        [jax.ShapeDtypeStruct(shape, BF16), jax.ShapeDtypeStruct(shape, F32)],
        flops=keep.size,
        moved=9 * keep.size,
    )


def derive(gate, up_val, dhidden):
    sigma = jax.nn.sigmoid(gate)
    return (
        (gate * sigma * up_val).astype(BF16),
        (dhidden * up_val * sigma * (1.0 + gate * (1.0 - sigma))).astype(BF16),
        (dhidden * gate * sigma).astype(BF16),
    )


def activate(line, keep, got):
    def kernel(keep_ref, got_ref, out_ref):
        sums = [keep_ref[k] + got_ref[k].astype(F32) for k in range(3)]
        for k, value in enumerate(derive(*sums)):
            out_ref[k] = value

    return line.call(
        kernel,
        [keep, got],
        [VMEM, VMEM],
        [VMEM],
        [jax.ShapeDtypeStruct(keep.shape, BF16)],
        flops=4 * keep.size,
        moved=8 * keep.size,
        turns=keep.size,
    )[0]


def activate_whole(line, sums):
    rows, wide = sums.shape
    hidden = wide // 3

    def kernel(sums_ref, out_ref):
        parts = [sums_ref[:, k * hidden:(k + 1) * hidden] for k in range(3)]
        for k, value in enumerate(derive(*parts)):
            out_ref[:, k * hidden:(k + 1) * hidden] = value

    return line.call(
        kernel,
        [sums],
        [VMEM],
        [VMEM],
        [jax.ShapeDtypeStruct(sums.shape, BF16)],
        flops=4 * sums.size,
        moved=6 * sums.size,
        turns=sums.size,
    )[0]


def piece_specs(pieces, hidden, which):
    specs = []
    for piece in pieces:
        if piece.ndim == 3:
            specs.append(pl.BlockSpec((1, piece.shape[1], TILE), lambda i: (which, 0, i)))
        else:
            first = which * (hidden // TILE)
            specs.append(pl.BlockSpec((piece.shape[0], TILE), lambda i: (0, first + i)))
    return specs


def tall(refs):
    return jnp.concatenate([ref[0] if len(ref.shape) == 3 else ref[...] for ref in refs], axis=0)


def results(line, flips, pieces, weights):
    gate_w, up_w, down_w = weights
    width, hidden = gate_w.shape
    rows = 2 * BLOCK
    count = len(pieces)

    def kernel(flip_ref, *refs):
        parts = [refs[k * count:(k + 1) * count] for k in range(3)]
        gate_ref, up_ref, down_ref, out0, out1, mixed_sum, input_sum = refs[3 * count:]
        step = pl.program_id(0)

        @pl.when(step == 0)
        def _():
            mixed_sum[...] = jnp.zeros_like(mixed_sum)
            input_sum[...] = jnp.zeros_like(input_sum)

        mixed_sum[...] += dot(tall(parts[0]), down_ref[...])
        input_sum[...] += dot_cols(tall(parts[1]), gate_ref[...]) + dot_cols(tall(parts[2]), up_ref[...])

        @pl.when(step == pl.num_programs(0) - 1)
        def _():
            for j, out in enumerate((out0, out1)):
                back = order_matrix(flip_ref[j], True)
                here = slice(j * BLOCK, (j + 1) * BLOCK)
                out[:, :width] = dot(back, mixed_sum[here].astype(BF16)).astype(BF16)
                out[:, width:] = dot(back, input_sum[here].astype(BF16)).astype(BF16)

    specs = [spec for which in range(3) for spec in piece_specs(pieces, hidden, which)]
    return line.call(
        kernel,
        [flips, *pieces, *pieces, *pieces, *map(far, weights)],
        [SMEM, *specs]
        + [
            pl.BlockSpec((width, TILE), lambda i: (0, i)),
            pl.BlockSpec((width, TILE), lambda i: (0, i)),
            pl.BlockSpec((TILE, width), lambda i: (i, 0)),
        ],
        [pl.BlockSpec((BLOCK, 2 * width), lambda i: (0, 0))] * 2,
        [jax.ShapeDtypeStruct((BLOCK, 2 * width), BF16)] * 2,
        flops=6 * rows * width * hidden,
        moved=6 * width * hidden + 6 * rows * hidden,
        grid=(hidden // TILE,),
        scratch=[pltpu.VMEM((rows, width), F32)] * 2,
    )


def weight_grad(line, which, rows, pieces, hidden):
    width = rows[0].shape[1] // 2
    count = len(rows)
    tokens = sum(r.shape[0] for r in rows)
    side = 1 if which == 0 else 0

    def down(*refs):
        cotangent = jnp.concatenate([r[...] for r in refs[:count]], axis=0)
        refs[-1][...] = dot_rows(tall(refs[count:-1]), cotangent).astype(BF16)

    def inward(*refs):
        out_ref, turned = refs[-2:]

        @pl.when(pl.program_id(0) == 0)
        def _():
            turned[...] = jnp.concatenate([r[...] for r in refs[:count]], axis=0).T

        out_ref[...] = dot(turned[...], tall(refs[count:-2])).astype(BF16)

    if which == 0:
        kernel, out, block, scratch = down, (hidden, width), pl.BlockSpec((TILE, width), lambda i: (i, 0)), []
    else:
        kernel, out, block = inward, (width, hidden), pl.BlockSpec((width, TILE), lambda i: (0, i))
        scratch = [pltpu.VMEM((width, tokens), BF16)]
    return line.call(
        kernel,
        [*map(far, rows), *pieces],
        [pl.BlockSpec((r.shape[0], width), lambda i: (0, side)) for r in rows] + piece_specs(pieces, hidden, which),
        [block],
        [hbm(out, BF16)],
        flops=2 * tokens * width * hidden,
        moved=2 * (tokens + width) * hidden,
        grid=(hidden // TILE,),
        scratch=scratch,
        vmem=32,
    )[0]


def vector(*values):
    return jnp.stack([jnp.asarray(v, jnp.int32) for v in values])


def whole_stream(line, blocks_at, weights, finish):
    blocks = [blocks_at[owner] for owner in WHOLE]
    sums = whole_terms(line, blocks, weights)
    sums = lax.psum_scatter(sums, "row", scatter_dimension=0, tiled=True)
    yield
    pieces = [lax.all_gather(activate_whole(line, sums), "row", axis=0, tiled=True)]
    yield
    parts = results(line, vector(0, 0), pieces, weights)
    finish(WHOLE, [jnp.concatenate(blocks, axis=0)], pieces, parts)


def halved_stream(line, blocks_at, weights, finish, bits, owners, early, late):
    (a, b), (c, d) = early, late
    flips = vector(bits[a] * 4 + bits[b] * 2 + bits[c], bits[b] * 4 + bits[a] * 2 + bits[c])
    rows, send0, keep0, send1, keep1 = halved_terms(line, [blocks_at[o] for o in owners], flips, weights)
    got0, got1 = exchange(send0, a), exchange(send1, b)
    yield
    send0, keep0 = add_rows(line, [keep0], [got0])
    got0 = exchange(send0, b)
    yield
    send1, keep1 = add_rows(line, [keep1], [got1])
    got1 = exchange(send1, a)
    yield
    send, keep = add_rows(line, [keep0, keep1], [got0, got1])
    got = exchange(send, c)
    yield
    send, keep = add_cols(line, vector(bits[d]), keep, got)
    got = exchange(send, d)
    yield
    near = activate(line, keep, got)
    got = exchange(near, d)
    upper = bits[d] == 1
    near = jnp.concatenate([jnp.where(upper, got, near), jnp.where(upper, near, got)], axis=2)
    got = exchange(near, c)
    near0 = jnp.concatenate([near[:, :GROUP], got[:, :GROUP]], axis=1)
    near1 = jnp.concatenate([near[:, GROUP:], got[:, GROUP:]], axis=1)
    near0 = jnp.concatenate([near0, exchange(near0, b)], axis=1)
    near1 = jnp.concatenate([near1, exchange(near1, a)], axis=1)
    pieces = [near0, exchange(near0, a), near1, exchange(near1, b)]
    yield
    parts = results(line, flips, pieces, weights)
    finish(owners, [rows], pieces, parts)


def on_device(tokens, cotangent, gate_w, up_w, down_w):
    width, hidden = gate_w.shape
    weights = (gate_w, up_w, down_w)
    bits = label_bits()
    blocks_at = {0: jnp.concatenate([tokens, cotangent], axis=1)}
    for distance in (1, 2, 3, 4):
        blocks_at[distance] = along_col(blocks_at[distance - 1], 1)
        if distance < 4:
            blocks_at[-distance] = along_col(blocks_at[1 - distance], -1)

    line = Line()
    all_rows, all_pieces, terms = [], [], []

    def finish(owners, rows, pieces, parts):
        all_rows.extend(rows)
        all_pieces.extend(pieces)
        for owner, part in zip(owners, parts):
            terms.append(along_col(part, -owner) if owner else part)

    streams = {"W": whole_stream(line, blocks_at, weights, finish)}
    for index, plan in enumerate(HALVED):
        streams[str(index)] = halved_stream(line, blocks_at, weights, finish, bits, *plan)
    for name in ORDER:
        next(streams[name], None)

    down_term = weight_grad(line, 0, all_rows, all_pieces, hidden)
    down_other = lax.ppermute(down_term, "dp", [(0, 1), (1, 0)])
    gate_term = weight_grad(line, 1, all_rows, all_pieces, hidden)
    gate_other = lax.ppermute(gate_term, "dp", [(0, 1), (1, 0)])
    up_term = weight_grad(line, 2, all_rows, all_pieces, hidden)
    up_other = lax.ppermute(up_term, "dp", [(0, 1), (1, 0)])

    def both(left, right):
        return (left.astype(F32) + right.astype(F32)).astype(BF16)

    sums = sum(term.astype(F32) for term in terms)
    return (
        sums[:, :width].astype(BF16),
        sums[:, width:].astype(BF16),
        both(gate_term, gate_other),
        both(up_term, up_other),
        both(down_term, down_other),
    )


def solution(mesh):
    specs = (
        P(("dp", "col"), "row"),
        P(("dp", "col"), "row"),
        P("row", "col"),
        P("row", "col"),
        P("col", "row"),
    )
    return jax.shard_map(on_device, mesh=mesh, in_specs=specs, out_specs=specs, check_vma=False)
```

```python
import jax
import jax.numpy as jnp
from jax import lax
from jax.experimental import pallas as pl
from jax.experimental.pallas import tpu as pltpu
from jax.sharding import PartitionSpec as P

F32 = jnp.float32
BF16 = jnp.bfloat16

ROW_PAIRS = (
    [(i, (i // 4) * 4 + ((i % 4) ^ 1)) for i in range(16)],
    [(i, (i // 4) * 4 + (3 - i % 4)) for i in range(16)],
    [(i, ((i // 4) ^ 1) * 4 + i % 4) for i in range(16)],
    [(i, (3 - i // 4) * 4 + i % 4) for i in range(16)],
)

STREAMS = (
    ((0, 1), (0, 2, 1, 3), (2, 0, 3, 1)),
    ((-1, 2), (1, 3, 0, 2), (3, 1, 2, 0)),
    ((-2, 3), (0, 2, 1, 3), (2, 0, 3, 1)),
    ((-3, 4), (1, 3, 0, 2), (3, 1, 2, 0)),
)

ORDER = "0120310210320131223301021" "3d2gu3"

BLOCK = 128
TILE = 256
GROUP = 16
VMEM = pl.BlockSpec(memory_space=pltpu.VMEM)
SMEM = pl.BlockSpec(memory_space=pltpu.SMEM)
ANY = pl.BlockSpec(memory_space=pl.ANY)


class Line:
    def __init__(self):
        self.last = None

    def call(self, kernel, args, in_specs, out_shape, scratch=(), vmem=12):
        inputs = len(args)
        skip = 0 if self.last is None else 1

        def body(*refs):
            kernel(*refs[:inputs], *refs[inputs + skip:])

        out = pl.pallas_call(
            body,
            in_specs=list(in_specs) + [ANY] * skip,
            out_specs=[VMEM] * len(out_shape),
            out_shape=out_shape,
            scratch_shapes=scratch,
            compiler_params=pltpu.CompilerParams(vmem_limit_bytes=vmem << 20),
            cost_estimate=pl.CostEstimate(flops=1, bytes_accessed=1, transcendentals=0),
        )(*args, *([self.last] if skip else []))
        self.last = out[0]
        return out


def exchange(value, orders, step):
    pairs = [(p * 16 + i, p * 16 + j) for p in range(2) for i, j in ROW_PAIRS[orders[p][step]]]
    return lax.ppermute(value, ("dp", "row"), pairs)


def along_col(value, distance):
    return lax.ppermute(value, "col", [(i, (i - distance) % 8) for i in range(8)])


def label_bits(orders):
    index = lax.axis_index("row")
    x, y = index // 4, index % 4
    bits = ((y >> 1) ^ (y & 1), y >> 1, (x >> 1) ^ (x & 1), x >> 1)
    first = lax.axis_index("dp") == 0
    return [jnp.where(first, bits[i], bits[j]) for i, j in zip(*orders)]


def vector(*values):
    return jnp.stack([jnp.asarray(v, jnp.int32) for v in values])


def order_matrix(flip, which, inverse):
    rows = 2 * BLOCK
    shape = (BLOCK, rows) if inverse else (rows, BLOCK)
    local = lax.broadcasted_iota(jnp.int32, shape, 1 if inverse else 0)
    plain = lax.broadcasted_iota(jnp.int32, shape, 0 if inverse else 1)
    wanted = (((local >> 5) ^ flip) << 4) + (local & 15)
    hit = (wanted == plain) & (((local >> 4) & 1) == which)
    return jnp.where(hit, 1.0, 0.0).astype(BF16)


def dot(left, right):
    return jnp.dot(left, right, preferred_element_type=F32)


def dot_cols(left, right):
    return lax.dot_general(left, right, (((1,), (1,)), ((), ())), preferred_element_type=F32)


def dot_rows(left, right):
    return lax.dot_general(left, right, (((0,), (0,)), ((), ())), preferred_element_type=F32)


def tiles(extent):
    return [slice(start, start + TILE) for start in range(0, extent, TILE)]


def stage_weights(line, weights):
    def kernel(*refs):
        copies = [pltpu.make_async_copy(refs[k], refs[3 + k], refs[6 + k]) for k in range(3)]
        for copy in copies:
            copy.start()
        for copy in copies:
            copy.wait()

    return line.call(
        kernel,
        [pltpu.with_memory_space_constraint(w, pltpu.HBM) for w in weights],
        [pl.BlockSpec(memory_space=pltpu.HBM)] * 3,
        [pltpu.VMEM(w.shape, w.dtype) for w in weights],
        scratch=[pltpu.SemaphoreType.DMA] * 3,
    )


def terms(line, flip, blocks, weights):
    width, hidden = weights[0].shape

    def kernel(flip_ref, first, second, gate_ref, up_ref, down_ref, rows_ref, send, keep):
        rows_ref[...] = (
            dot(order_matrix(flip_ref[0], 0, False), first[...]) + dot(order_matrix(flip_ref[0], 1, False), second[...])
        ).astype(BF16)
        inputs, upstream = rows_ref[:, :width], rows_ref[:, width:]
        for cols in tiles(hidden):
            values = (dot(inputs, gate_ref[:, cols]), dot(inputs, up_ref[:, cols]), dot_cols(upstream, down_ref[cols]))
            for index, value in enumerate(values):
                keep[index, :, cols] = value[:BLOCK]
                send[index, :, cols] = value[BLOCK:].astype(BF16)

    shape = (3, BLOCK, hidden)
    return line.call(
        kernel,
        [flip, *blocks, *weights],
        [SMEM] + [VMEM] * 5,
        [pltpu.VMEM((2 * BLOCK, 2 * width), BF16), pltpu.VMEM(shape, BF16), pltpu.VMEM(shape, F32)],
    )


def add_rows(line, keep, got):
    _, rows, hidden = keep.shape
    half = rows // 2

    def kernel(keep_ref, got_ref, send_ref, next_ref):
        for k in range(3):
            next_ref[k] = keep_ref[k, :half] + got_ref[k, :half].astype(F32)
            send_ref[k] = (keep_ref[k, half:] + got_ref[k, half:].astype(F32)).astype(BF16)

    shape = (3, half, hidden)
    return line.call(kernel, [keep, got], [VMEM, VMEM], [pltpu.VMEM(shape, BF16), pltpu.VMEM(shape, F32)])


def add_cols(line, bit, keep, got):
    _, rows, hidden = keep.shape
    half = hidden // 2

    def kernel(bit_ref, keep_ref, got_ref, send_ref, next_ref):
        upper = bit_ref[0] == 1
        for k in range(3):
            low = keep_ref[k, :, :half] + got_ref[k, :, :half].astype(F32)
            high = keep_ref[k, :, half:] + got_ref[k, :, half:].astype(F32)
            next_ref[k] = jnp.where(upper, high, low)
            send_ref[k] = jnp.where(upper, low, high).astype(BF16)

    shape = (3, rows, half)
    return line.call(kernel, [bit, keep, got], [SMEM, VMEM, VMEM], [pltpu.VMEM(shape, BF16), pltpu.VMEM(shape, F32)])


def activate(line, keep, got):
    def kernel(keep_ref, got_ref, out_ref):
        gate, up_val, dhidden = [keep_ref[k] + got_ref[k].astype(F32) for k in range(3)]
        sigma = jax.nn.sigmoid(gate)
        out_ref[0] = (gate * sigma * up_val).astype(BF16)
        out_ref[1] = (dhidden * up_val * sigma * (1.0 + gate * (1.0 - sigma))).astype(BF16)
        out_ref[2] = (dhidden * gate * sigma).astype(BF16)

    return line.call(kernel, [keep, got], [VMEM, VMEM], [pltpu.VMEM(keep.shape, BF16)])[0]


def results(line, flip, near, far, weights):
    width, hidden = weights[0].shape

    def kernel(flip_ref, near_ref, far_ref, gate_ref, up_ref, down_ref, out0, out1):
        mixed = [jnp.zeros((BLOCK, width), F32)] * 2
        input_grad = [jnp.zeros((BLOCK, width), F32)] * 2
        for cols in tiles(hidden):
            for h, piece in enumerate((near_ref, far_ref)):
                mixed[h] += dot(piece[0, :, cols], down_ref[cols])
                input_grad[h] += dot_cols(piece[1, :, cols], gate_ref[:, cols])
                input_grad[h] += dot_cols(piece[2, :, cols], up_ref[:, cols])
        both = jnp.concatenate(
            [jnp.concatenate([m, g], axis=1) for m, g in zip(mixed, input_grad)], axis=0
        ).astype(BF16)
        for j, out in enumerate((out0, out1)):
            out[...] = dot(order_matrix(flip_ref[0], j, True), both).astype(BF16)

    return line.call(
        kernel,
        [flip, near, far, *weights],
        [SMEM] + [VMEM] * 5,
        [pltpu.VMEM((BLOCK, 2 * width), BF16)] * 2,
    )


def gather_sums(line, total, parts):
    def kernel(*refs):
        value = refs[0][...].astype(F32)
        for ref in refs[1:-1]:
            value += ref[...].astype(F32)
        refs[-1][...] = value

    args = ([] if total is None else [total]) + parts
    return line.call(kernel, args, [VMEM] * len(args), [pltpu.VMEM(parts[0].shape, F32)])[0]


def weight_grad(line, which, rows, pieces):
    width = rows[0].shape[1] // 2
    hidden = pieces[0].shape[2]
    count = len(rows)

    def kernel(*refs):
        row_refs, piece_refs, out_ref = refs[:count], refs[count:-1], refs[-1]
        side = slice(width, None) if which == 0 else slice(0, width)
        outer = jnp.concatenate([r[:, side] for r in row_refs], axis=0)
        if which:
            outer = outer.T
        for cols in tiles(hidden):
            inner = jnp.concatenate([p[which, :, cols] for p in piece_refs], axis=0)
            if which:
                out_ref[:, cols] = dot(outer, inner).astype(BF16)
            else:
                out_ref[cols] = dot_rows(inner, outer).astype(BF16)

    out = (width, hidden) if which else (hidden, width)
    args = [*rows, *pieces]
    return line.call(kernel, args, [VMEM] * len(args), [pltpu.VMEM(out, BF16)])[0]


def stream(line, plan, blocks_at, weights, state):
    owners, *orders = plan
    bits = label_bits(orders)
    flip, last = vector(bits[0] * 4 + bits[1] * 2 + bits[2]), vector(bits[3])
    rows, send, keep = terms(line, flip, [blocks_at[o] for o in owners], weights)
    got = exchange(send, orders, 0)
    yield
    send, keep = add_rows(line, keep, got)
    got = exchange(send, orders, 1)
    yield
    send, keep = add_rows(line, keep, got)
    got = exchange(send, orders, 2)
    yield
    send, keep = add_cols(line, last, keep, got)
    got = exchange(send, orders, 3)
    yield
    near = activate(line, keep, got)
    got = exchange(near, orders, 3)
    upper = bits[3] == 1
    near = jnp.concatenate([jnp.where(upper, got, near), jnp.where(upper, near, got)], axis=2)
    near = jnp.concatenate([near, exchange(near, orders, 2)], axis=1)
    near = jnp.concatenate([near, exchange(near, orders, 1)], axis=1)
    far = exchange(near, orders, 0)
    yield
    parts = results(line, flip, near, far, weights)
    parts = [along_col(part, -owner) if owner else part for owner, part in zip(owners, parts)]
    state["rows"].append(rows)
    state["pieces"] += [near, far]
    yield
    state["total"] = gather_sums(line, state["total"], parts)


def on_device(tokens, cotangent, *weights):
    width = tokens.shape[1]
    blocks_at = {0: jnp.concatenate([tokens, cotangent], axis=1)}
    for distance in (1, 2, 3, 4):
        blocks_at[distance] = along_col(blocks_at[distance - 1], 1)
        if distance < 4:
            blocks_at[-distance] = along_col(blocks_at[1 - distance], -1)

    line = Line()
    weights = stage_weights(line, weights)
    state = {"rows": [], "pieces": [], "total": None}
    streams = [stream(line, plan, blocks_at, weights, state) for plan in STREAMS]
    grads, others = [], []
    for name in ORDER:
        if name in "dgu":
            grads.append(weight_grad(line, "dgu".index(name), state["rows"], state["pieces"]))
            others.append(lax.ppermute(grads[-1], "dp", [(0, 1), (1, 0)]))
        else:
            next(streams[int(name)], None)

    down_grad, gate_grad, up_grad = [
        (left.astype(F32) + right.astype(F32)).astype(BF16) for left, right in zip(grads, others)
    ]
    total = state["total"]
    return total[:, :width].astype(BF16), total[:, width:].astype(BF16), gate_grad, up_grad, down_grad


def solution(mesh):
    specs = (
        P(("dp", "col"), "row"),
        P(("dp", "col"), "row"),
        P("row", "col"),
        P("row", "col"),
        P("col", "row"),
    )
    return jax.shard_map(on_device, mesh=mesh, in_specs=specs, out_specs=specs, check_vma=False)
```

```python
import jax
import jax.numpy as jnp
from jax import lax
from jax.experimental import pallas as pl
from jax.experimental.pallas import tpu as pltpu
from jax.sharding import PartitionSpec as P

F32 = jnp.float32
BF16 = jnp.bfloat16

ROW_PAIRS = (
    [(i, (i // 4) * 4 + ((i % 4) ^ 1)) for i in range(16)],
    [(i, (i // 4) * 4 + (3 - i % 4)) for i in range(16)],
    [(i, ((i // 4) ^ 1) * 4 + i % 4) for i in range(16)],
    [(i, (3 - i // 4) * 4 + i % 4) for i in range(16)],
)

STREAMS = (
    ((1, -1), (1, 2, 0, 3), (0, 3, 1, 2)),
    ((2, -2), (2, 0, 3, 1), (3, 1, 2, 0)),
    ((3, -3), (0, 3, 2, 1), (1, 2, 3, 0)),
    ((0, 4), (3, 1, 2, 0), (2, 0, 3, 1)),
)

ORDER = "0123010210321032103210321302132" "031x2x3idy"

BLOCK = 128
TILE = 256
GROUP = 16
VMEM = pl.BlockSpec(memory_space=pltpu.VMEM)
SMEM = pl.BlockSpec(memory_space=pltpu.SMEM)
ANY = pl.BlockSpec(memory_space=pl.ANY)


class Line:
    def __init__(self):
        self.last = None

    def call(self, kernel, args, in_specs, out_shape, us, scratch=(), vmem=6):
        inputs = len(args)
        skip = 0 if self.last is None else 1

        def body(*refs):
            kernel(*refs[:inputs], *refs[inputs + skip:])

        out = pl.pallas_call(
            body,
            in_specs=list(in_specs) + [ANY] * skip,
            out_specs=[VMEM] * len(out_shape),
            out_shape=out_shape,
            scratch_shapes=scratch,
            compiler_params=pltpu.CompilerParams(vmem_limit_bytes=vmem << 20),
            cost_estimate=pl.CostEstimate(flops=int(us * 1.1e10), bytes_accessed=int(us * 3.5e7), transcendentals=0),
        )(*args, *([self.last] if skip else []))
        self.last = out[0]
        return out


def exchange(value, orders, step):
    pairs = [(p * 16 + i, p * 16 + j) for p in range(2) for i, j in ROW_PAIRS[orders[p][step]]]
    return lax.ppermute(value, ("dp", "row"), pairs)


def along_col(value, distance):
    return lax.ppermute(value, "col", [(i, (i - distance) % 8) for i in range(8)])


def label_bits(orders):
    index = lax.axis_index("row")
    x, y = index // 4, index % 4
    bits = ((y >> 1) ^ (y & 1), y >> 1, (x >> 1) ^ (x & 1), x >> 1)
    first = lax.axis_index("dp") == 0
    return [jnp.where(first, bits[i], bits[j]) for i, j in zip(*orders)]


def vector(*values):
    return jnp.stack([jnp.asarray(v, jnp.int32) for v in values])


def order_matrix(flip, which, inverse):
    rows = 2 * BLOCK
    shape = (BLOCK, rows) if inverse else (rows, BLOCK)
    local = lax.broadcasted_iota(jnp.int32, shape, 1 if inverse else 0)
    plain = lax.broadcasted_iota(jnp.int32, shape, 0 if inverse else 1)
    wanted = (((local >> 5) ^ flip) << 4) + (local & 15)
    hit = (wanted == plain) & (((local >> 4) & 1) == which)
    return jnp.where(hit, 1.0, 0.0).astype(BF16)


def dot(left, right):
    return jnp.dot(left, right, preferred_element_type=F32)


def dot_cols(left, right):
    return lax.dot_general(left, right, (((1,), (1,)), ((), ())), preferred_element_type=F32)


def dot_rows(left, right):
    return lax.dot_general(left, right, (((0,), (0,)), ((), ())), preferred_element_type=F32)


def tiles(extent):
    return [slice(start, start + TILE) for start in range(0, extent, TILE)]


def near_core(value):
    return pltpu.with_memory_space_constraint(value, pltpu.VMEM)


def pack(line, tokens, cotangent):
    rows, width = tokens.shape

    def kernel(tokens_ref, cotangent_ref, out_ref):
        out_ref[:, :width] = tokens_ref[...]
        out_ref[:, width:] = cotangent_ref[...]

    return line.call(kernel, [tokens, cotangent], [VMEM, VMEM], [pltpu.VMEM((rows, 2 * width), BF16)], us=0.1)[0]


def stage_weights(line, weights):
    def kernel(*refs):
        copies = [pltpu.make_async_copy(refs[k], refs[3 + k], refs[6 + k]) for k in range(3)]
        for copy in copies:
            copy.start()
        for copy in copies:
            copy.wait()

    return line.call(
        kernel,
        [pltpu.with_memory_space_constraint(w, pltpu.HBM) for w in weights],
        [pl.BlockSpec(memory_space=pltpu.HBM)] * 3,
        [pltpu.VMEM(w.shape, w.dtype) for w in weights],
        us=4.5,
        scratch=[pltpu.SemaphoreType.DMA] * 3,
    )


def terms(line, flip, blocks, weights):
    width, hidden = weights[0].shape

    def kernel(flip_ref, first, second, gate_ref, up_ref, down_ref, rows_ref, send, keep):
        rows_ref[...] = (
            dot(order_matrix(flip_ref[0], 0, False), first[...]) + dot(order_matrix(flip_ref[0], 1, False), second[...])
        ).astype(BF16)
        inputs, upstream = rows_ref[:, :width], rows_ref[:, width:]
        for cols in tiles(hidden):
            values = (dot(inputs, gate_ref[:, cols]), dot(inputs, up_ref[:, cols]), dot_cols(upstream, down_ref[cols]))
            for index, value in enumerate(values):
                keep[index, :, cols] = value[:BLOCK]
                send[index, :, cols] = value[BLOCK:].astype(BF16)

    shape = (3, BLOCK, hidden)
    return line.call(
        kernel,
        [flip, *blocks, *map(near_core, weights)],
        [SMEM] + [VMEM] * 5,
        [pltpu.VMEM((2 * BLOCK, 2 * width), BF16), pltpu.VMEM(shape, BF16), pltpu.VMEM(shape, F32)],
        us=3.0,
    )


def add_rows(line, keep, got, kept):
    _, rows, hidden = keep.shape
    half = rows // 2

    def kernel(keep_ref, got_ref, send_ref, next_ref):
        for k in range(3):
            next_ref[k] = (keep_ref[k, :half].astype(F32) + got_ref[k, :half].astype(F32)).astype(kept)
            send_ref[k] = (keep_ref[k, half:].astype(F32) + got_ref[k, half:].astype(F32)).astype(BF16)

    shape = (3, half, hidden)
    return line.call(kernel, [keep, got], [VMEM, VMEM], [pltpu.VMEM(shape, BF16), pltpu.VMEM(shape, kept)], us=rows / 75)


def add_cols(line, bit, keep, got):
    _, rows, hidden = keep.shape
    half = hidden // 2

    def kernel(bit_ref, keep_ref, got_ref, send_ref, next_ref):
        upper = bit_ref[0] == 1
        for k in range(3):
            low = keep_ref[k, :, :half] + got_ref[k, :, :half].astype(F32)
            high = keep_ref[k, :, half:] + got_ref[k, :, half:].astype(F32)
            next_ref[k] = jnp.where(upper, high, low)
            send_ref[k] = jnp.where(upper, low, high)

    shape = (3, rows, half)
    return line.call(kernel, [bit, keep, got], [SMEM, VMEM, VMEM], [pltpu.VMEM(shape, F32), pltpu.VMEM(shape, F32)], us=0.4)


def activate(line, keep, got):
    def kernel(keep_ref, got_ref, out_ref):
        gate, up_val, dhidden = [keep_ref[k] + got_ref[k] for k in range(3)]
        sigma = jax.nn.sigmoid(gate)
        out_ref[0] = (gate * sigma * up_val).astype(BF16)
        out_ref[1] = (dhidden * up_val * sigma * (1.0 + gate * (1.0 - sigma))).astype(BF16)
        out_ref[2] = (dhidden * gate * sigma).astype(BF16)

    return line.call(kernel, [keep, got], [VMEM, VMEM], [pltpu.VMEM(keep.shape, BF16)], us=0.7)[0]


def join_cols(line, bit, near, got):
    _, rows, half = near.shape

    def kernel(bit_ref, near_ref, got_ref, out_ref):
        upper = bit_ref[0] == 1
        for k in range(3):
            out_ref[k, :, :half] = jnp.where(upper, got_ref[k], near_ref[k])
            out_ref[k, :, half:] = jnp.where(upper, near_ref[k], got_ref[k])

    return line.call(kernel, [bit, near, got], [SMEM, VMEM, VMEM], [pltpu.VMEM((3, rows, 2 * half), BF16)], us=0.3)[0]


def join_rows(line, near, got):
    _, rows, hidden = near.shape

    def kernel(near_ref, got_ref, out_ref):
        out_ref[:, :rows] = near_ref[...]
        out_ref[:, rows:] = got_ref[...]

    return line.call(kernel, [near, got], [VMEM, VMEM], [pltpu.VMEM((3, 2 * rows, hidden), BF16)], us=0.3)[0]


def results(line, flip, near, far, weights):
    width, hidden = weights[0].shape

    def kernel(flip_ref, near_ref, far_ref, gate_ref, up_ref, down_ref, out0, out1):
        mixed = [jnp.zeros((BLOCK, width), F32)] * 2
        input_grad = [jnp.zeros((BLOCK, width), F32)] * 2
        for cols in tiles(hidden):
            for h, piece in enumerate((near_ref, far_ref)):
                mixed[h] += dot(piece[0, :, cols], down_ref[cols])
                input_grad[h] += dot_cols(piece[1, :, cols], gate_ref[:, cols])
                input_grad[h] += dot_cols(piece[2, :, cols], up_ref[:, cols])
        both = jnp.concatenate(
            [jnp.concatenate([m, g], axis=1) for m, g in zip(mixed, input_grad)], axis=0
        ).astype(BF16)
        for j, out in enumerate((out0, out1)):
            out[...] = dot(order_matrix(flip_ref[0], j, True), both).astype(BF16)

    return line.call(
        kernel,
        [flip, near, far, *map(near_core, weights)],
        [SMEM] + [VMEM] * 5,
        [pltpu.VMEM((BLOCK, 2 * width), BF16)] * 2,
        us=0.3,
    )


def gather_sums(line, total, parts, us):
    def kernel(*refs):
        value = refs[0][...].astype(F32)
        for ref in refs[1:-1]:
            value += ref[...].astype(F32)
        refs[-1][...] = value

    args = ([] if total is None else [total]) + parts
    return line.call(kernel, args, [VMEM] * len(args), [pltpu.VMEM(parts[0].shape, F32)], us=us)[0]


def down_term(line, rows, pieces):
    width = rows[0].shape[1] // 2
    hidden = pieces[0].shape[2]
    count = len(rows)

    def kernel(*refs):
        row_refs, piece_refs, out_ref = refs[:count], refs[count:-1], refs[-1]
        upstream = jnp.concatenate([r[:, width:] for r in row_refs], axis=0)
        for cols in tiles(hidden):
            out_ref[cols] = dot_rows(
                jnp.concatenate([p[0, :, cols] for p in piece_refs], axis=0), upstream
            ).astype(BF16)

    args = [*rows, *pieces]
    return line.call(kernel, args, [VMEM] * len(args), [pltpu.VMEM((hidden, width), BF16)], us=0.02)[0]


def inner_terms(line, rows, pieces):
    width = rows[0].shape[1] // 2
    hidden = pieces[0].shape[2]
    count = len(rows)

    def kernel(*refs):
        row_refs, piece_refs, out_ref = refs[:count], refs[count:-1], refs[-1]
        inputs = jnp.concatenate([r[:, :width] for r in row_refs], axis=0).T
        for which in (0, 1):
            for cols in tiles(hidden):
                grads = jnp.concatenate([p[1 + which, :, cols] for p in piece_refs], axis=0)
                out_ref[which, :, cols] = dot(inputs, grads).astype(BF16)

    args = [*rows, *pieces]
    return line.call(kernel, args, [VMEM] * len(args), [pltpu.VMEM((2, width, hidden), BF16)], us=0.02)[0]


def stream(line, plan, blocks_at, weights, state):
    owners, *orders = plan
    bits = label_bits(orders)
    flip, last = vector(bits[0] * 4 + bits[1] * 2 + bits[2]), vector(bits[3])
    rows, send, keep = terms(line, flip, [blocks_at[o] for o in owners], weights)
    got = exchange(send, orders, 0)
    yield
    send, keep = add_rows(line, keep, got, F32)
    got = exchange(send, orders, 1)
    yield
    send, keep = add_rows(line, keep, got, F32)
    got = exchange(send, orders, 2)
    yield
    send, keep = add_cols(line, last, keep, got)
    got = exchange(send, orders, 3)
    yield
    near = activate(line, keep, got)
    got = exchange(near, orders, 3)
    yield
    near = join_cols(line, last, near, got)
    got = exchange(near, orders, 2)
    yield
    near = join_rows(line, near, got)
    got = exchange(near, orders, 1)
    yield
    near = join_rows(line, near, got)
    far = exchange(near, orders, 0)
    state["rows"].append(rows)
    state["pieces"] += [near, far]
    yield
    parts = results(line, flip, near, far, weights)
    parts = [along_col(part, -owner) if owner else part for owner, part in zip(owners, parts)]
    state["parts"].append(parts)


def on_device(tokens, cotangent, *weights):
    width = tokens.shape[1]
    line = Line()
    blocks_at = {0: pack(line, tokens, cotangent)}
    for distance in (1, 2, 3, 4):
        blocks_at[distance] = along_col(blocks_at[distance - 1], 1)
        if distance < 4:
            blocks_at[-distance] = along_col(blocks_at[1 - distance], -1)

    weights = stage_weights(line, weights)
    state = {"rows": [], "pieces": [], "parts": []}
    streams = [stream(line, plan, blocks_at, weights, state) for plan in STREAMS]
    grads, total = {}, None
    for name in ORDER:
        if name in "xyz":
            count = "xyz".index(name) + 1
            waiting = sum(state["parts"][:count], [])
            del state["parts"][:count]
            total = gather_sums(line, total, waiting, 0.3 if name == "x" else 10.0)
            continue
        if name in "id":
            mine = (inner_terms if name == "i" else down_term)(line, state["rows"], state["pieces"])
            grads[name] = (mine, lax.ppermute(mine, "dp", [(0, 1), (1, 0)]))
        else:
            next(streams[int(name)], None)

    def both(left, right):
        return (left.astype(F32) + right.astype(F32)).astype(BF16)

    mine, other = grads["i"]
    return (
        total[:, :width].astype(BF16),
        total[:, width:].astype(BF16),
        both(mine[0], other[0]),
        both(mine[1], other[1]),
        both(*grads["d"]),
    )


def solution(mesh):
    specs = (
        P(("dp", "col"), "row"),
        P(("dp", "col"), "row"),
        P("row", "col"),
        P("row", "col"),
        P("col", "row"),
    )
    return jax.shard_map(on_device, mesh=mesh, in_specs=specs, out_specs=specs, check_vma=False)
```

```python
import jax
import jax.numpy as jnp
from jax import lax
from jax.experimental import pallas as pl
from jax.experimental.pallas import tpu as pltpu
from jax.sharding import PartitionSpec as P

F32 = jnp.float32
BF16 = jnp.bfloat16

ROW_PAIRS = (
    [(i, (i // 4) * 4 + ((i % 4) ^ 1)) for i in range(16)],
    [(i, (i // 4) * 4 + (3 - i % 4)) for i in range(16)],
    [(i, ((i // 4) ^ 1) * 4 + i % 4) for i in range(16)],
    [(i, (3 - i // 4) * 4 + i % 4) for i in range(16)],
)

STREAMS = (
    ((1, -1), (1, 2, 0, 3), (0, 3, 1, 2)),
    ((2, -2), (2, 0, 3, 1), (3, 1, 2, 0)),
    ((3, -3), (0, 3, 2, 1), (1, 2, 3, 0)),
    ((0, 4), (3, 1, 2, 0), (2, 0, 3, 1)),
)

ORDER = "0123010210321032103210321302132" "031x2x3idy"

BLOCK = 128
TILE = 256
GROUP = 16
VMEM = pl.BlockSpec(memory_space=pltpu.VMEM)
SMEM = pl.BlockSpec(memory_space=pltpu.SMEM)
ANY = pl.BlockSpec(memory_space=pl.ANY)


class Line:
    def __init__(self):
        self.last = None

    def call(self, kernel, args, in_specs, out_shape, us, scratch=(), vmem=6):
        inputs = len(args)
        skip = 0 if self.last is None else 1

        def body(*refs):
            kernel(*refs[:inputs], *refs[inputs + skip:])

        out = pl.pallas_call(
            body,
            in_specs=list(in_specs) + [ANY] * skip,
            out_specs=[VMEM] * len(out_shape),
            out_shape=out_shape,
            scratch_shapes=scratch,
            compiler_params=pltpu.CompilerParams(vmem_limit_bytes=vmem << 20),
            cost_estimate=pl.CostEstimate(flops=int(us * 1.1e10), bytes_accessed=int(us * 3.5e7), transcendentals=0),
        )(*args, *([self.last] if skip else []))
        self.last = out[0]
        return out


def exchange(value, orders, step):
    pairs = [(p * 16 + i, p * 16 + j) for p in range(2) for i, j in ROW_PAIRS[orders[p][step]]]
    return lax.ppermute(value, ("dp", "row"), pairs)


def along_col(value, distance):
    return lax.ppermute(value, "col", [(i, (i - distance) % 8) for i in range(8)])


def label_bits(orders):
    index = lax.axis_index("row")
    x, y = index // 4, index % 4
    bits = ((y >> 1) ^ (y & 1), y >> 1, (x >> 1) ^ (x & 1), x >> 1)
    first = lax.axis_index("dp") == 0
    return [jnp.where(first, bits[i], bits[j]) for i, j in zip(*orders)]


def vector(*values):
    return jnp.stack([jnp.asarray(v, jnp.int32) for v in values])


def order_matrix(flip, which, inverse):
    rows = 2 * BLOCK
    shape = (BLOCK, rows) if inverse else (rows, BLOCK)
    local = lax.broadcasted_iota(jnp.int32, shape, 1 if inverse else 0)
    plain = lax.broadcasted_iota(jnp.int32, shape, 0 if inverse else 1)
    wanted = (((local >> 5) ^ flip) << 4) + (local & 15)
    hit = (wanted == plain) & (((local >> 4) & 1) == which)
    return jnp.where(hit, 1.0, 0.0).astype(BF16)


def dot(left, right):
    return jnp.dot(left, right, preferred_element_type=F32)


def dot_cols(left, right):
    return lax.dot_general(left, right, (((1,), (1,)), ((), ())), preferred_element_type=F32)


def dot_rows(left, right):
    return lax.dot_general(left, right, (((0,), (0,)), ((), ())), preferred_element_type=F32)


def tiles(extent):
    return [slice(start, start + TILE) for start in range(0, extent, TILE)]


def near_core(value):
    return pltpu.with_memory_space_constraint(value, pltpu.VMEM)


def pack(line, tokens, cotangent):
    rows, width = tokens.shape

    def kernel(tokens_ref, cotangent_ref, out_ref):
        out_ref[:, :width] = tokens_ref[...]
        out_ref[:, width:] = cotangent_ref[...]

    return line.call(kernel, [tokens, cotangent], [VMEM, VMEM], [pltpu.VMEM((rows, 2 * width), BF16)], us=0.1)[0]


def stage_weights(line, weights):
    def kernel(*refs):
        copies = [pltpu.make_async_copy(refs[k], refs[3 + k], refs[6 + k]) for k in range(3)]
        for copy in copies:
            copy.start()
        for copy in copies:
            copy.wait()

    return line.call(
        kernel,
        [pltpu.with_memory_space_constraint(w, pltpu.HBM) for w in weights],
        [pl.BlockSpec(memory_space=pltpu.HBM)] * 3,
        [pltpu.VMEM(w.shape, w.dtype) for w in weights],
        us=4.5,
        scratch=[pltpu.SemaphoreType.DMA] * 3,
    )


def terms(line, flip, blocks, weights):
    width, hidden = weights[0].shape

    def kernel(flip_ref, first, second, gate_ref, up_ref, down_ref, rows_ref, send, keep):
        rows_ref[...] = (
            dot(order_matrix(flip_ref[0], 0, False), first[...]) + dot(order_matrix(flip_ref[0], 1, False), second[...])
        ).astype(BF16)
        inputs, upstream = rows_ref[:, :width], rows_ref[:, width:]
        for cols in tiles(hidden):
            values = (dot(inputs, gate_ref[:, cols]), dot(inputs, up_ref[:, cols]), dot_cols(upstream, down_ref[cols]))
            for index, value in enumerate(values):
                keep[index, :, cols] = value[:BLOCK]
                send[index, :, cols] = value[BLOCK:].astype(BF16)

    shape = (3, BLOCK, hidden)
    return line.call(
        kernel,
        [flip, *blocks, *map(near_core, weights)],
        [SMEM] + [VMEM] * 5,
        [pltpu.VMEM((2 * BLOCK, 2 * width), BF16), pltpu.VMEM(shape, BF16), pltpu.VMEM(shape, F32)],
        us=3.0,
    )


def add_rows(line, keep, got, kept):
    _, rows, hidden = keep.shape
    half = rows // 2

    def kernel(keep_ref, got_ref, send_ref, next_ref):
        for k in range(3):
            next_ref[k] = (keep_ref[k, :half].astype(F32) + got_ref[k, :half].astype(F32)).astype(kept)
            send_ref[k] = (keep_ref[k, half:].astype(F32) + got_ref[k, half:].astype(F32)).astype(BF16)

    shape = (3, half, hidden)
    return line.call(kernel, [keep, got], [VMEM, VMEM], [pltpu.VMEM(shape, BF16), pltpu.VMEM(shape, kept)], us=rows / 75)


def add_cols(line, bit, keep, got):
    _, rows, hidden = keep.shape
    half = hidden // 2

    def kernel(bit_ref, keep_ref, got_ref, send_ref, next_ref):
        upper = bit_ref[0] == 1
        for k in range(3):
            low = keep_ref[k, :, :half] + got_ref[k, :, :half].astype(F32)
            high = keep_ref[k, :, half:] + got_ref[k, :, half:].astype(F32)
            next_ref[k] = jnp.where(upper, high, low)
            send_ref[k] = jnp.where(upper, low, high)

    shape = (3, rows, half)
    return line.call(kernel, [bit, keep, got], [SMEM, VMEM, VMEM], [pltpu.VMEM(shape, F32), pltpu.VMEM(shape, F32)], us=0.4)


def activate(line, keep, got):
    def kernel(keep_ref, got_ref, out_ref):
        gate, up_val, dhidden = [keep_ref[k] + got_ref[k] for k in range(3)]
        sigma = jax.nn.sigmoid(gate)
        out_ref[0] = (gate * sigma * up_val).astype(BF16)
        out_ref[1] = (dhidden * up_val * sigma * (1.0 + gate * (1.0 - sigma))).astype(BF16)
        out_ref[2] = (dhidden * gate * sigma).astype(BF16)

    return line.call(kernel, [keep, got], [VMEM, VMEM], [pltpu.VMEM(keep.shape, BF16)], us=0.7)[0]


def join_cols(line, bit, near, got):
    _, rows, half = near.shape

    def kernel(bit_ref, near_ref, got_ref, out_ref):
        upper = bit_ref[0] == 1
        for k in range(3):
            out_ref[k, :, :half] = jnp.where(upper, got_ref[k], near_ref[k])
            out_ref[k, :, half:] = jnp.where(upper, near_ref[k], got_ref[k])

    return line.call(kernel, [bit, near, got], [SMEM, VMEM, VMEM], [pltpu.VMEM((3, rows, 2 * half), BF16)], us=0.3)[0]


def join_rows(line, near, got):
    _, rows, hidden = near.shape

    def kernel(near_ref, got_ref, out_ref):
        out_ref[:, :rows] = near_ref[...]
        out_ref[:, rows:] = got_ref[...]

    return line.call(kernel, [near, got], [VMEM, VMEM], [pltpu.VMEM((3, 2 * rows, hidden), BF16)], us=0.8)[0]


def results(line, flip, near, far, weights):
    width, hidden = weights[0].shape

    def kernel(flip_ref, near_ref, far_ref, gate_ref, up_ref, down_ref, out0, out1):
        mixed = input_grad = jnp.zeros((2 * BLOCK, width), F32)
        for cols in tiles(hidden):
            parts = [jnp.concatenate([near_ref[k, :, cols], far_ref[k, :, cols]], axis=0) for k in range(3)]
            mixed += dot(parts[0], down_ref[cols])
            input_grad += dot_cols(parts[1], gate_ref[:, cols]) + dot_cols(parts[2], up_ref[:, cols])
        both = jnp.concatenate([mixed, input_grad], axis=1).astype(BF16)
        for j, out in enumerate((out0, out1)):
            out[...] = dot(order_matrix(flip_ref[0], j, True), both).astype(BF16)

    return line.call(
        kernel,
        [flip, near, far, *map(near_core, weights)],
        [SMEM] + [VMEM] * 5,
        [pltpu.VMEM((BLOCK, 2 * width), BF16)] * 2,
        us=0.3,
    )


def gather_sums(line, total, parts, us):
    def kernel(*refs):
        value = refs[0][...].astype(F32)
        for ref in refs[1:-1]:
            value += ref[...].astype(F32)
        refs[-1][...] = value

    args = ([] if total is None else [total]) + parts
    return line.call(kernel, args, [VMEM] * len(args), [pltpu.VMEM(parts[0].shape, F32)], us=us)[0]


def down_term(line, rows, pieces):
    width = rows[0].shape[1] // 2
    hidden = pieces[0].shape[2]
    count = len(rows)

    def kernel(*refs):
        row_refs, piece_refs, out_ref = refs[:count], refs[count:-1], refs[-1]
        upstream = jnp.concatenate([r[:, width:] for r in row_refs], axis=0)
        for cols in tiles(hidden):
            out_ref[cols] = dot_rows(
                jnp.concatenate([p[0, :, cols] for p in piece_refs], axis=0), upstream
            ).astype(BF16)

    args = [*rows, *pieces]
    return line.call(kernel, args, [VMEM] * len(args), [pltpu.VMEM((hidden, width), BF16)], us=0.02)[0]


def inner_terms(line, rows, pieces):
    width = rows[0].shape[1] // 2
    hidden = pieces[0].shape[2]
    count = len(rows)

    def kernel(*refs):
        row_refs, piece_refs, out_ref = refs[:count], refs[count:-1], refs[-1]
        inputs = jnp.concatenate([r[:, :width] for r in row_refs], axis=0).T
        for which in (0, 1):
            for cols in tiles(hidden):
                grads = jnp.concatenate([p[1 + which, :, cols] for p in piece_refs], axis=0)
                out_ref[which, :, cols] = dot(inputs, grads).astype(BF16)

    args = [*rows, *pieces]
    return line.call(kernel, args, [VMEM] * len(args), [pltpu.VMEM((2, width, hidden), BF16)], us=0.02)[0]


def stream(line, plan, blocks_at, weights, state):
    owners, *orders = plan
    bits = label_bits(orders)
    flip, last = vector(bits[0] * 4 + bits[1] * 2 + bits[2]), vector(bits[3])
    rows, send, keep = terms(line, flip, [blocks_at[o] for o in owners], weights)
    got = exchange(send, orders, 0)
    yield
    send, keep = add_rows(line, keep, got, F32)
    got = exchange(send, orders, 1)
    yield
    send, keep = add_rows(line, keep, got, F32)
    got = exchange(send, orders, 2)
    yield
    send, keep = add_cols(line, last, keep, got)
    got = exchange(send, orders, 3)
    yield
    near = activate(line, keep, got)
    got = exchange(near, orders, 3)
    yield
    near = join_cols(line, last, near, got)
    got = exchange(near, orders, 2)
    yield
    near = join_rows(line, near, got)
    got = exchange(near, orders, 1)
    yield
    near = join_rows(line, near, got)
    far = exchange(near, orders, 0)
    state["rows"].append(rows)
    state["pieces"] += [near, far]
    yield
    parts = results(line, flip, near, far, weights)
    parts = [along_col(part, -owner) if owner else part for owner, part in zip(owners, parts)]
    state["parts"].append(parts)


def on_device(tokens, cotangent, *weights):
    width = tokens.shape[1]
    line = Line()
    blocks_at = {0: pack(line, tokens, cotangent)}
    for distance in (1, 2, 3, 4):
        blocks_at[distance] = along_col(blocks_at[distance - 1], 1)
        if distance < 4:
            blocks_at[-distance] = along_col(blocks_at[1 - distance], -1)

    weights = stage_weights(line, weights)
    state = {"rows": [], "pieces": [], "parts": []}
    streams = [stream(line, plan, blocks_at, weights, state) for plan in STREAMS]
    grads, total = {}, None
    for name in ORDER:
        if name in "xyz":
            count = "xyz".index(name) + 1
            waiting = sum(state["parts"][:count], [])
            del state["parts"][:count]
            total = gather_sums(line, total, waiting, 0.3 if name == "x" else 10.0)
            continue
        if name in "id":
            mine = (inner_terms if name == "i" else down_term)(line, state["rows"], state["pieces"])
            grads[name] = (mine, lax.ppermute(mine, "dp", [(0, 1), (1, 0)]))
        else:
            next(streams[int(name)], None)

    def both(left, right):
        return (left.astype(F32) + right.astype(F32)).astype(BF16)

    mine, other = grads["i"]
    return (
        total[:, :width].astype(BF16),
        total[:, width:].astype(BF16),
        both(mine[0], other[0]),
        both(mine[1], other[1]),
        both(*grads["d"]),
    )


def solution(mesh):
    specs = (
        P(("dp", "col"), "row"),
        P(("dp", "col"), "row"),
        P("row", "col"),
        P("row", "col"),
        P("col", "row"),
    )
    return jax.shard_map(on_device, mesh=mesh, in_specs=specs, out_specs=specs, check_vma=False)
```

```python
import jax
import jax.numpy as jnp
from jax import lax
from jax.experimental import pallas as pl
from jax.experimental.pallas import tpu as pltpu
from jax.sharding import PartitionSpec as P

F32 = jnp.float32
BF16 = jnp.bfloat16

ROW_PAIRS = (
    [(i, (i // 4) * 4 + ((i % 4) ^ 1)) for i in range(16)],
    [(i, (i // 4) * 4 + (3 - i % 4)) for i in range(16)],
    [(i, ((i // 4) ^ 1) * 4 + i % 4) for i in range(16)],
    [(i, (3 - i // 4) * 4 + i % 4) for i in range(16)],
)

STREAMS = (
    ((1, -1), (1, 2, 0, 3), (0, 3, 1, 2)),
    ((2, -2), (2, 0, 3, 1), (3, 1, 2, 0)),
    ((3, -3), (0, 3, 2, 1), (1, 2, 3, 0)),
    ((0, 4), (0, 2, 1, 3), (1, 3, 0, 2)),
)

ORDER = "0123010210321032103210321302132" "031x2x3idy"

BLOCK = 128
TILE = 256
GROUP = 16
VMEM = pl.BlockSpec(memory_space=pltpu.VMEM)
SMEM = pl.BlockSpec(memory_space=pltpu.SMEM)
ANY = pl.BlockSpec(memory_space=pl.ANY)


class Line:
    def __init__(self):
        self.last = None

    def call(self, kernel, args, in_specs, out_shape, us, scratch=(), vmem=6):
        inputs = len(args)
        skip = 0 if self.last is None else 1

        def body(*refs):
            kernel(*refs[:inputs], *refs[inputs + skip:])

        out = pl.pallas_call(
            body,
            in_specs=list(in_specs) + [ANY] * skip,
            out_specs=[VMEM] * len(out_shape),
            out_shape=out_shape,
            scratch_shapes=scratch,
            compiler_params=pltpu.CompilerParams(vmem_limit_bytes=vmem << 20),
            cost_estimate=pl.CostEstimate(flops=int(us * 1.1e10), bytes_accessed=int(us * 3.5e7), transcendentals=0),
        )(*args, *([self.last] if skip else []))
        self.last = out[0]
        return out


def exchange(value, orders, step):
    pairs = [(p * 16 + i, p * 16 + j) for p in range(2) for i, j in ROW_PAIRS[orders[p][step]]]
    return lax.ppermute(value, ("dp", "row"), pairs)


def along_col(value, distance):
    return lax.ppermute(value, "col", [(i, (i - distance) % 8) for i in range(8)])


def label_bits(orders):
    index = lax.axis_index("row")
    x, y = index // 4, index % 4
    bits = ((y >> 1) ^ (y & 1), y >> 1, (x >> 1) ^ (x & 1), x >> 1)
    first = lax.axis_index("dp") == 0
    return [jnp.where(first, bits[i], bits[j]) for i, j in zip(*orders)]


def vector(*values):
    return jnp.stack([jnp.asarray(v, jnp.int32) for v in values])


def order_matrix(flip, which, inverse):
    rows = 2 * BLOCK
    shape = (BLOCK, rows) if inverse else (rows, BLOCK)
    local = lax.broadcasted_iota(jnp.int32, shape, 1 if inverse else 0)
    plain = lax.broadcasted_iota(jnp.int32, shape, 0 if inverse else 1)
    wanted = (((local >> 5) ^ flip) << 4) + (local & 15)
    hit = (wanted == plain) & (((local >> 4) & 1) == which)
    return jnp.where(hit, 1.0, 0.0).astype(BF16)


def dot(left, right):
    return jnp.dot(left, right, preferred_element_type=F32)


def dot_cols(left, right):
    return lax.dot_general(left, right, (((1,), (1,)), ((), ())), preferred_element_type=F32)


def dot_rows(left, right):
    return lax.dot_general(left, right, (((0,), (0,)), ((), ())), preferred_element_type=F32)


def tiles(extent):
    return [slice(start, start + TILE) for start in range(0, extent, TILE)]


def near_core(value):
    return pltpu.with_memory_space_constraint(value, pltpu.VMEM)


def pack(line, tokens, cotangent):
    rows, width = tokens.shape

    def kernel(tokens_ref, cotangent_ref, out_ref, first, second):
        copies = [
            pltpu.make_async_copy(tokens_ref, out_ref.at[:, :width], first),
            pltpu.make_async_copy(cotangent_ref, out_ref.at[:, width:], second),
        ]
        for copy in copies:
            copy.start()
        for copy in copies:
            copy.wait()

    return line.call(
        kernel,
        [pltpu.with_memory_space_constraint(x, pltpu.HBM) for x in (tokens, cotangent)],
        [pl.BlockSpec(memory_space=pltpu.HBM)] * 2,
        [pltpu.VMEM((rows, 2 * width), BF16)],
        us=0.1,
        scratch=[pltpu.SemaphoreType.DMA] * 2,
    )[0]


def stage_weights(line, weights):
    def kernel(*refs):
        copies = [pltpu.make_async_copy(refs[k], refs[3 + k], refs[6 + k]) for k in range(3)]
        for copy in copies:
            copy.start()
        for copy in copies:
            copy.wait()

    return line.call(
        kernel,
        [pltpu.with_memory_space_constraint(w, pltpu.HBM) for w in weights],
        [pl.BlockSpec(memory_space=pltpu.HBM)] * 3,
        [pltpu.VMEM(w.shape, w.dtype) for w in weights],
        us=4.5,
        scratch=[pltpu.SemaphoreType.DMA] * 3,
    )


def terms(line, flip, blocks, weights):
    width, hidden = weights[0].shape

    def kernel(flip_ref, first, second, gate_ref, up_ref, down_ref, rows_ref, send, keep):
        rows_ref[...] = (
            dot(order_matrix(flip_ref[0], 0, False), first[...]) + dot(order_matrix(flip_ref[0], 1, False), second[...])
        ).astype(BF16)
        inputs, upstream = rows_ref[:, :width], rows_ref[:, width:]
        for cols in tiles(hidden):
            values = (dot(inputs, gate_ref[:, cols]), dot(inputs, up_ref[:, cols]), dot_cols(upstream, down_ref[cols]))
            for index, value in enumerate(values):
                keep[index, :, cols] = value[:BLOCK]
                send[index, :, cols] = value[BLOCK:].astype(BF16)

    shape = (3, BLOCK, hidden)
    return line.call(
        kernel,
        [flip, *blocks, *map(near_core, weights)],
        [SMEM] + [VMEM] * 5,
        [pltpu.VMEM((2 * BLOCK, 2 * width), BF16), pltpu.VMEM(shape, BF16), pltpu.VMEM(shape, F32)],
        us=3.0,
    )


def add_rows(line, keep, got, kept):
    _, rows, hidden = keep.shape
    half = rows // 2

    def kernel(keep_ref, got_ref, send_ref, next_ref):
        for k in range(3):
            next_ref[k] = (keep_ref[k, :half].astype(F32) + got_ref[k, :half].astype(F32)).astype(kept)
            send_ref[k] = (keep_ref[k, half:].astype(F32) + got_ref[k, half:].astype(F32)).astype(BF16)

    shape = (3, half, hidden)
    return line.call(kernel, [keep, got], [VMEM, VMEM], [pltpu.VMEM(shape, BF16), pltpu.VMEM(shape, kept)], us=rows / 75)


def add_cols(line, bit, keep, got):
    _, rows, hidden = keep.shape
    half = hidden // 2

    def kernel(bit_ref, keep_ref, got_ref, send_ref, next_ref):
        upper = bit_ref[0] == 1
        for k in range(3):
            low = keep_ref[k, :, :half] + got_ref[k, :, :half].astype(F32)
            high = keep_ref[k, :, half:] + got_ref[k, :, half:].astype(F32)
            next_ref[k] = jnp.where(upper, high, low)
            send_ref[k] = jnp.where(upper, low, high)

    shape = (3, rows, half)
    return line.call(kernel, [bit, keep, got], [SMEM, VMEM, VMEM], [pltpu.VMEM(shape, F32), pltpu.VMEM(shape, F32)], us=0.4)


def activate(line, keep, got):
    def kernel(keep_ref, got_ref, out_ref):
        gate, up_val, dhidden = [keep_ref[k] + got_ref[k] for k in range(3)]
        sigma = jax.nn.sigmoid(gate)
        out_ref[0] = (gate * sigma * up_val).astype(BF16)
        out_ref[1] = (dhidden * up_val * sigma * (1.0 + gate * (1.0 - sigma))).astype(BF16)
        out_ref[2] = (dhidden * gate * sigma).astype(BF16)

    return line.call(kernel, [keep, got], [VMEM, VMEM], [pltpu.VMEM(keep.shape, BF16)], us=0.7)[0]


def join_cols(line, bit, near, got):
    _, rows, half = near.shape

    def kernel(bit_ref, near_ref, got_ref, out_ref):
        upper = bit_ref[0] == 1
        for k in range(3):
            out_ref[k, :, :half] = jnp.where(upper, got_ref[k], near_ref[k])
            out_ref[k, :, half:] = jnp.where(upper, near_ref[k], got_ref[k])

    return line.call(kernel, [bit, near, got], [SMEM, VMEM, VMEM], [pltpu.VMEM((3, rows, 2 * half), BF16)], us=0.3)[0]


def join_rows(line, near, got):
    _, rows, hidden = near.shape

    def kernel(near_ref, got_ref, out_ref):
        out_ref[:, :rows] = near_ref[...]
        out_ref[:, rows:] = got_ref[...]

    return line.call(kernel, [near, got], [VMEM, VMEM], [pltpu.VMEM((3, 2 * rows, hidden), BF16)], us=0.8)[0]


def results(line, flip, near, far, weights, us):
    width, hidden = weights[0].shape

    def kernel(flip_ref, near_ref, far_ref, gate_ref, up_ref, down_ref, out0, out1):
        mixed = input_grad = jnp.zeros((2 * BLOCK, width), F32)
        for cols in tiles(hidden):
            parts = [jnp.concatenate([near_ref[k, :, cols], far_ref[k, :, cols]], axis=0) for k in range(3)]
            mixed += dot(parts[0], down_ref[cols])
            input_grad += dot_cols(parts[1], gate_ref[:, cols]) + dot_cols(parts[2], up_ref[:, cols])
        both = jnp.concatenate([mixed, input_grad], axis=1).astype(BF16)
        for j, out in enumerate((out0, out1)):
            out[...] = dot(order_matrix(flip_ref[0], j, True), both).astype(BF16)

    return line.call(
        kernel,
        [flip, near, far, *map(near_core, weights)],
        [SMEM] + [VMEM] * 5,
        [pltpu.VMEM((BLOCK, 2 * width), BF16)] * 2,
        us=us,
    )


def gather_sums(line, total, parts, us):
    def kernel(*refs):
        value = refs[0][...].astype(F32)
        for ref in refs[1:-1]:
            value += ref[...].astype(F32)
        refs[-1][...] = value

    args = ([] if total is None else [total]) + parts
    return line.call(kernel, args, [VMEM] * len(args), [pltpu.VMEM(parts[0].shape, F32)], us=us)[0]


def down_term(line, rows, pieces):
    width = rows[0].shape[1] // 2
    hidden = pieces[0].shape[2]
    count = len(rows)

    def kernel(*refs):
        row_refs, piece_refs, out_ref = refs[:count], refs[count:-1], refs[-1]
        upstream = jnp.concatenate([r[:, width:] for r in row_refs], axis=0)
        for cols in tiles(hidden):
            out_ref[cols] = dot_rows(
                jnp.concatenate([p[0, :, cols] for p in piece_refs], axis=0), upstream
            ).astype(BF16)

    args = [*rows, *pieces]
    return line.call(kernel, args, [VMEM] * len(args), [pltpu.VMEM((hidden, width), BF16)], us=0.02)[0]


def inner_terms(line, rows, pieces):
    width = rows[0].shape[1] // 2
    hidden = pieces[0].shape[2]
    count = len(rows)

    def kernel(*refs):
        row_refs, piece_refs, out_ref = refs[:count], refs[count:-1], refs[-1]
        inputs = jnp.concatenate([r[:, :width] for r in row_refs], axis=0).T
        for which in (0, 1):
            for cols in tiles(hidden):
                grads = jnp.concatenate([p[1 + which, :, cols] for p in piece_refs], axis=0)
                out_ref[which, :, cols] = dot(inputs, grads).astype(BF16)

    args = [*rows, *pieces]
    return line.call(kernel, args, [VMEM] * len(args), [pltpu.VMEM((2, width, hidden), BF16)], us=0.02)[0]


def stream(line, plan, blocks_at, weights, state):
    owners, *orders = plan
    bits = label_bits(orders)
    flip, last = vector(bits[0] * 4 + bits[1] * 2 + bits[2]), vector(bits[3])
    rows, send, keep = terms(line, flip, [blocks_at[o] for o in owners], weights)
    got = exchange(send, orders, 0)
    yield
    send, keep = add_rows(line, keep, got, F32)
    got = exchange(send, orders, 1)
    yield
    send, keep = add_rows(line, keep, got, F32)
    got = exchange(send, orders, 2)
    yield
    send, keep = add_cols(line, last, keep, got)
    got = exchange(send, orders, 3)
    yield
    near = activate(line, keep, got)
    got = exchange(near, orders, 3)
    yield
    near = join_cols(line, last, near, got)
    got = exchange(near, orders, 2)
    yield
    near = join_rows(line, near, got)
    got = exchange(near, orders, 1)
    yield
    near = join_rows(line, near, got)
    far = exchange(near, orders, 0)
    state["rows"].append(rows)
    state["pieces"] += [near, far]
    yield
    parts = results(line, flip, near, far, weights, 1.0 if owners == STREAMS[1][0] else 0.3)
    parts = [along_col(part, -owner) if owner else part for owner, part in zip(owners, parts)]
    state["parts"].append(parts)


def on_device(tokens, cotangent, *weights):
    width = tokens.shape[1]
    line = Line()
    blocks_at = {0: pack(line, tokens, cotangent)}
    for distance in (1, 2, 3, 4):
        blocks_at[distance] = along_col(blocks_at[distance - 1], 1)
        if distance < 4:
            blocks_at[-distance] = along_col(blocks_at[1 - distance], -1)

    weights = stage_weights(line, weights)
    state = {"rows": [], "pieces": [], "parts": []}
    streams = [stream(line, plan, blocks_at, weights, state) for plan in STREAMS]
    grads, total = {}, None
    for name in ORDER:
        if name in "xyz":
            count = "xyz".index(name) + 1
            waiting = sum(state["parts"][:count], [])
            del state["parts"][:count]
            total = gather_sums(line, total, waiting, 0.3 if name == "x" else 10.0)
            continue
        if name in "id":
            mine = (inner_terms if name == "i" else down_term)(line, state["rows"], state["pieces"])
            grads[name] = (mine, lax.ppermute(mine, "dp", [(0, 1), (1, 0)]))
        else:
            next(streams[int(name)], None)

    def both(left, right):
        return (left.astype(F32) + right.astype(F32)).astype(BF16)

    mine, other = grads["i"]
    return (
        total[:, :width].astype(BF16),
        total[:, width:].astype(BF16),
        both(mine[0], other[0]),
        both(mine[1], other[1]),
        both(*grads["d"]),
    )


def solution(mesh):
    specs = (
        P(("dp", "col"), "row"),
        P(("dp", "col"), "row"),
        P("row", "col"),
        P("row", "col"),
        P("col", "row"),
    )
    return jax.shard_map(on_device, mesh=mesh, in_specs=specs, out_specs=specs, check_vma=False)
```

```python
import jax
import jax.numpy as jnp
from jax import lax
from jax.experimental import pallas as pl
from jax.experimental.pallas import tpu as pltpu
from jax.sharding import PartitionSpec as P

F32 = jnp.float32
BF16 = jnp.bfloat16

ROW_PAIRS = (
    [(i, (i // 4) * 4 + ((i % 4) ^ 1)) for i in range(16)],
    [(i, (i // 4) * 4 + (3 - i % 4)) for i in range(16)],
    [(i, ((i // 4) ^ 1) * 4 + i % 4) for i in range(16)],
    [(i, (3 - i // 4) * 4 + i % 4) for i in range(16)],
)

STREAMS = (
    ((1, -1), (1, 2, 0, 3), (0, 3, 1, 2)),
    ((2, -2), (2, 0, 3, 1), (3, 1, 2, 0)),
    ((3, -3), (0, 3, 2, 1), (1, 2, 3, 0)),
    ((0, 4), (0, 2, 1, 3), (1, 3, 0, 2)),
)

ORDER = "0123010210321032103210321302132031x2pq3xidy"

BLOCK = 128
TILE = 256
GROUP = 16
VMEM = pl.BlockSpec(memory_space=pltpu.VMEM)
SMEM = pl.BlockSpec(memory_space=pltpu.SMEM)
ANY = pl.BlockSpec(memory_space=pl.ANY)


class Line:
    def __init__(self):
        self.last = None

    def call(self, kernel, args, in_specs, out_shape, us, scratch=(), vmem=6):
        inputs = len(args)
        skip = 0 if self.last is None else 1

        def body(*refs):
            kernel(*refs[:inputs], *refs[inputs + skip:])

        out = pl.pallas_call(
            body,
            in_specs=list(in_specs) + [ANY] * skip,
            out_specs=[VMEM] * len(out_shape),
            out_shape=out_shape,
            scratch_shapes=scratch,
            compiler_params=pltpu.CompilerParams(vmem_limit_bytes=vmem << 20),
            cost_estimate=pl.CostEstimate(flops=int(us * 1.1e10), bytes_accessed=int(us * 3.5e7), transcendentals=0),
        )(*args, *([self.last] if skip else []))
        self.last = out[0]
        return out


def exchange(value, orders, step):
    pairs = [(p * 16 + i, p * 16 + j) for p in range(2) for i, j in ROW_PAIRS[orders[p][step]]]
    return lax.ppermute(value, ("dp", "row"), pairs)


def along_col(value, distance):
    return lax.ppermute(value, "col", [(i, (i - distance) % 8) for i in range(8)])


def label_bits(orders):
    index = lax.axis_index("row")
    x, y = index // 4, index % 4
    bits = ((y >> 1) ^ (y & 1), y >> 1, (x >> 1) ^ (x & 1), x >> 1)
    first = lax.axis_index("dp") == 0
    return [jnp.where(first, bits[i], bits[j]) for i, j in zip(*orders)]


def vector(*values):
    return jnp.stack([jnp.asarray(v, jnp.int32) for v in values])


def order_matrix(flip, which, inverse):
    rows = 2 * BLOCK
    shape = (BLOCK, rows) if inverse else (rows, BLOCK)
    local = lax.broadcasted_iota(jnp.int32, shape, 1 if inverse else 0)
    plain = lax.broadcasted_iota(jnp.int32, shape, 0 if inverse else 1)
    wanted = (((local >> 5) ^ flip) << 4) + (local & 15)
    hit = (wanted == plain) & (((local >> 4) & 1) == which)
    return jnp.where(hit, 1.0, 0.0).astype(BF16)


def dot(left, right):
    return jnp.dot(left, right, preferred_element_type=F32)


def dot_cols(left, right):
    return lax.dot_general(left, right, (((1,), (1,)), ((), ())), preferred_element_type=F32)


def dot_rows(left, right):
    return lax.dot_general(left, right, (((0,), (0,)), ((), ())), preferred_element_type=F32)


def tiles(extent):
    return [slice(start, start + TILE) for start in range(0, extent, TILE)]


def near_core(value):
    return pltpu.with_memory_space_constraint(value, pltpu.VMEM)


def pack(line, tokens, cotangent):
    rows, width = tokens.shape

    def kernel(tokens_ref, cotangent_ref, out_ref, first, second):
        copies = [
            pltpu.make_async_copy(tokens_ref, out_ref.at[:, :width], first),
            pltpu.make_async_copy(cotangent_ref, out_ref.at[:, width:], second),
        ]
        for copy in copies:
            copy.start()
        for copy in copies:
            copy.wait()

    return line.call(
        kernel,
        [pltpu.with_memory_space_constraint(x, pltpu.HBM) for x in (tokens, cotangent)],
        [pl.BlockSpec(memory_space=pltpu.HBM)] * 2,
        [pltpu.VMEM((rows, 2 * width), BF16)],
        us=0.1,
        scratch=[pltpu.SemaphoreType.DMA] * 2,
    )[0]


def stage_weights(line, weights):
    def kernel(*refs):
        copies = [pltpu.make_async_copy(refs[k], refs[3 + k], refs[6 + k]) for k in range(3)]
        for copy in copies:
            copy.start()
        for copy in copies:
            copy.wait()

    return line.call(
        kernel,
        [pltpu.with_memory_space_constraint(w, pltpu.HBM) for w in weights],
        [pl.BlockSpec(memory_space=pltpu.HBM)] * 3,
        [pltpu.VMEM(w.shape, w.dtype) for w in weights],
        us=4.5,
        scratch=[pltpu.SemaphoreType.DMA] * 3,
    )


def terms(line, flip, blocks, weights):
    width, hidden = weights[0].shape

    def kernel(flip_ref, first, second, gate_ref, up_ref, down_ref, rows_ref, send, keep):
        rows_ref[...] = (
            dot(order_matrix(flip_ref[0], 0, False), first[...]) + dot(order_matrix(flip_ref[0], 1, False), second[...])
        ).astype(BF16)
        inputs, upstream = rows_ref[:, :width], rows_ref[:, width:]
        for cols in tiles(hidden):
            values = (dot(inputs, gate_ref[:, cols]), dot(inputs, up_ref[:, cols]), dot_cols(upstream, down_ref[cols]))
            for index, value in enumerate(values):
                keep[index, :, cols] = value[:BLOCK]
                send[index, :, cols] = value[BLOCK:].astype(BF16)

    shape = (3, BLOCK, hidden)
    return line.call(
        kernel,
        [flip, *blocks, *map(near_core, weights)],
        [SMEM] + [VMEM] * 5,
        [pltpu.VMEM((2 * BLOCK, 2 * width), BF16), pltpu.VMEM(shape, BF16), pltpu.VMEM(shape, F32)],
        us=3.0,
    )


def add_rows(line, keep, got, kept):
    _, rows, hidden = keep.shape
    half = rows // 2

    def kernel(keep_ref, got_ref, send_ref, next_ref):
        for k in range(3):
            next_ref[k] = (keep_ref[k, :half].astype(F32) + got_ref[k, :half].astype(F32)).astype(kept)
            send_ref[k] = (keep_ref[k, half:].astype(F32) + got_ref[k, half:].astype(F32)).astype(BF16)

    shape = (3, half, hidden)
    return line.call(kernel, [keep, got], [VMEM, VMEM], [pltpu.VMEM(shape, BF16), pltpu.VMEM(shape, kept)], us=rows / 75)


def add_cols(line, bit, keep, got):
    _, rows, hidden = keep.shape
    half = hidden // 2

    def kernel(bit_ref, keep_ref, got_ref, send_ref, next_ref):
        upper = bit_ref[0] == 1
        for k in range(3):
            low = keep_ref[k, :, :half] + got_ref[k, :, :half].astype(F32)
            high = keep_ref[k, :, half:] + got_ref[k, :, half:].astype(F32)
            next_ref[k] = jnp.where(upper, high, low)
            send_ref[k] = jnp.where(upper, low, high)

    shape = (3, rows, half)
    return line.call(kernel, [bit, keep, got], [SMEM, VMEM, VMEM], [pltpu.VMEM(shape, F32), pltpu.VMEM(shape, F32)], us=0.4)


def activate(line, keep, got):
    def kernel(keep_ref, got_ref, out_ref):
        gate, up_val, dhidden = [keep_ref[k] + got_ref[k] for k in range(3)]
        sigma = jax.nn.sigmoid(gate)
        out_ref[0] = (gate * sigma * up_val).astype(BF16)
        out_ref[1] = (dhidden * up_val * sigma * (1.0 + gate * (1.0 - sigma))).astype(BF16)
        out_ref[2] = (dhidden * gate * sigma).astype(BF16)

    return line.call(kernel, [keep, got], [VMEM, VMEM], [pltpu.VMEM(keep.shape, BF16)], us=0.7)[0]


def join_cols(line, bit, near, got):
    _, rows, half = near.shape

    def kernel(bit_ref, near_ref, got_ref, out_ref):
        upper = bit_ref[0] == 1
        for k in range(3):
            out_ref[k, :, :half] = jnp.where(upper, got_ref[k], near_ref[k])
            out_ref[k, :, half:] = jnp.where(upper, near_ref[k], got_ref[k])

    return line.call(kernel, [bit, near, got], [SMEM, VMEM, VMEM], [pltpu.VMEM((3, rows, 2 * half), BF16)], us=0.3)[0]


def join_rows(line, near, got):
    _, rows, hidden = near.shape

    def kernel(near_ref, got_ref, out_ref):
        out_ref[:, :rows] = near_ref[...]
        out_ref[:, rows:] = got_ref[...]

    return line.call(kernel, [near, got], [VMEM, VMEM], [pltpu.VMEM((3, 2 * rows, hidden), BF16)], us=0.8)[0]


def results(line, flip, near, far, weights, us):
    width, hidden = weights[0].shape

    def kernel(flip_ref, near_ref, far_ref, gate_ref, up_ref, down_ref, out0, out1):
        mixed = input_grad = jnp.zeros((2 * BLOCK, width), F32)
        for cols in tiles(hidden):
            parts = [jnp.concatenate([near_ref[k, :, cols], far_ref[k, :, cols]], axis=0) for k in range(3)]
            mixed += dot(parts[0], down_ref[cols])
            input_grad += dot_cols(parts[1], gate_ref[:, cols]) + dot_cols(parts[2], up_ref[:, cols])
        both = jnp.concatenate([mixed, input_grad], axis=1).astype(BF16)
        for j, out in enumerate((out0, out1)):
            out[...] = dot(order_matrix(flip_ref[0], j, True), both).astype(BF16)

    return line.call(
        kernel,
        [flip, near, far, *map(near_core, weights)],
        [SMEM] + [VMEM] * 5,
        [pltpu.VMEM((BLOCK, 2 * width), BF16)] * 2,
        us=us,
    )


def gather_sums(line, total, parts, us):
    def kernel(*refs):
        value = refs[0][...].astype(F32)
        for ref in refs[1:-1]:
            value += ref[...].astype(F32)
        refs[-1][...] = value

    args = ([] if total is None else [total]) + parts
    return line.call(kernel, args, [VMEM] * len(args), [pltpu.VMEM(parts[0].shape, F32)], us=us)[0]


def down_term(line, rows, pieces, held, last):
    width = rows[0].shape[1] // 2
    hidden = pieces[0].shape[2]
    count = len(rows)
    parts = len(pieces)

    def kernel(*refs):
        row_refs, piece_refs, out_ref = refs[:count], refs[count:count + parts], refs[-1]
        upstream = jnp.concatenate([r[:, width:] for r in row_refs], axis=0)
        for cols in tiles(hidden):
            value = dot_rows(jnp.concatenate([p[0, :, cols] for p in piece_refs], axis=0), upstream)
            if held is not None:
                value += refs[count + parts][cols]
            out_ref[cols] = value.astype(out_ref.dtype)

    args = [*rows, *pieces] + ([] if held is None else [held])
    out = pltpu.VMEM((hidden, width), BF16 if last else F32)
    return line.call(kernel, args, [VMEM] * len(args), [out], us=0.02)[0]


def inner_terms(line, rows, pieces, held, last):
    width = rows[0].shape[1] // 2
    hidden = pieces[0].shape[2]
    count = len(rows)
    parts = len(pieces)

    def kernel(*refs):
        row_refs, piece_refs, out_ref = refs[:count], refs[count:count + parts], refs[-1]
        inputs = jnp.concatenate([r[:, :width] for r in row_refs], axis=0).T
        for which in (0, 1):
            for cols in tiles(hidden):
                grads = jnp.concatenate([p[1 + which, :, cols] for p in piece_refs], axis=0)
                value = dot(inputs, grads)
                if held is not None:
                    value += refs[count + parts][which, :, cols]
                out_ref[which, :, cols] = value.astype(out_ref.dtype)

    args = [*rows, *pieces] + ([] if held is None else [held])
    out = pltpu.VMEM((2, width, hidden), BF16 if last else F32)
    return line.call(kernel, args, [VMEM] * len(args), [out], us=0.02)[0]


def stream(line, plan, blocks_at, weights, state):
    owners, *orders = plan
    bits = label_bits(orders)
    flip, last = vector(bits[0] * 4 + bits[1] * 2 + bits[2]), vector(bits[3])
    rows, send, keep = terms(line, flip, [blocks_at[o] for o in owners], weights)
    got = exchange(send, orders, 0)
    yield
    send, keep = add_rows(line, keep, got, F32)
    got = exchange(send, orders, 1)
    yield
    send, keep = add_rows(line, keep, got, F32)
    got = exchange(send, orders, 2)
    yield
    send, keep = add_cols(line, last, keep, got)
    got = exchange(send, orders, 3)
    yield
    near = activate(line, keep, got)
    got = exchange(near, orders, 3)
    yield
    near = join_cols(line, last, near, got)
    got = exchange(near, orders, 2)
    yield
    near = join_rows(line, near, got)
    got = exchange(near, orders, 1)
    yield
    near = join_rows(line, near, got)
    far = exchange(near, orders, 0)
    state["rows"].append(rows)
    state["pieces"] += [near, far]
    yield
    parts = results(line, flip, near, far, weights, 1.0 if owners == STREAMS[1][0] else 0.3)
    parts = [along_col(part, -owner) if owner else part for owner, part in zip(owners, parts)]
    state["parts"].append(parts)


def on_device(tokens, cotangent, *weights):
    width = tokens.shape[1]
    line = Line()
    blocks_at = {0: pack(line, tokens, cotangent)}
    for distance in (1, 2, 3, 4):
        blocks_at[distance] = along_col(blocks_at[distance - 1], 1)
        if distance < 4:
            blocks_at[-distance] = along_col(blocks_at[1 - distance], -1)

    weights = stage_weights(line, weights)
    state = {"rows": [], "pieces": [], "parts": []}
    streams = [stream(line, plan, blocks_at, weights, state) for plan in STREAMS]
    grads, held, total = {}, {}, None
    for name in ORDER:
        if name in "xyz":
            count = "xyz".index(name) + 1
            waiting = sum(state["parts"][:count], [])
            del state["parts"][:count]
            total = gather_sums(line, total, waiting, 0.3 if name == "x" else 10.0)
            continue
        if name in "pq":
            make = inner_terms if name == "p" else down_term
            held[name] = make(line, state["rows"][:3], state["pieces"][:6], None, False)
        elif name in "id":
            make, first = (inner_terms, "p") if name == "i" else (down_term, "q")
            mine = make(line, state["rows"][3:], state["pieces"][6:], held[first], True)
            grads[name] = (mine, lax.ppermute(mine, "dp", [(0, 1), (1, 0)]))
        else:
            next(streams[int(name)], None)

    def both(left, right):
        return (left.astype(F32) + right.astype(F32)).astype(BF16)

    mine, other = grads["i"]
    return (
        total[:, :width].astype(BF16),
        total[:, width:].astype(BF16),
        both(mine[0], other[0]),
        both(mine[1], other[1]),
        both(*grads["d"]),
    )


def solution(mesh):
    specs = (
        P(("dp", "col"), "row"),
        P(("dp", "col"), "row"),
        P("row", "col"),
        P("row", "col"),
        P("col", "row"),
    )
    return jax.shard_map(on_device, mesh=mesh, in_specs=specs, out_specs=specs, check_vma=False)
```

```python
import jax
import jax.numpy as jnp
from jax import lax
from jax.experimental import pallas as pl
from jax.experimental.pallas import tpu as pltpu
from jax.sharding import PartitionSpec as P

F32 = jnp.float32
BF16 = jnp.bfloat16

ROW_PAIRS = (
    [(i, (i // 4) * 4 + ((i % 4) ^ 1)) for i in range(16)],
    [(i, (i // 4) * 4 + (3 - i % 4)) for i in range(16)],
    [(i, ((i // 4) ^ 1) * 4 + i % 4) for i in range(16)],
    [(i, (3 - i // 4) * 4 + i % 4) for i in range(16)],
)

STREAMS = (
    ((1, -1), (1, 2, 0, 3), (0, 3, 1, 2)),
    ((3, -3), (2, 0, 3, 1), (3, 1, 2, 0)),
    ((2, -2), (0, 3, 2, 1), (1, 2, 3, 0)),
    ((0, 4), (0, 2, 3, 1), (1, 3, 2, 0)),
)

ORDER = "0213010210321032103210321302312031x2pq3xidy"

BLOCK = 128
TILE = 256
GROUP = 16
VMEM = pl.BlockSpec(memory_space=pltpu.VMEM)
SMEM = pl.BlockSpec(memory_space=pltpu.SMEM)
ANY = pl.BlockSpec(memory_space=pl.ANY)


class Line:
    def __init__(self):
        self.last = None

    def call(self, kernel, args, in_specs, out_shape, us, scratch=(), vmem=6):
        inputs = len(args)
        skip = 0 if self.last is None else 1

        def body(*refs):
            kernel(*refs[:inputs], *refs[inputs + skip:])

        out = pl.pallas_call(
            body,
            in_specs=list(in_specs) + [ANY] * skip,
            out_specs=[VMEM] * len(out_shape),
            out_shape=out_shape,
            scratch_shapes=scratch,
            compiler_params=pltpu.CompilerParams(vmem_limit_bytes=vmem << 20),
            cost_estimate=pl.CostEstimate(flops=int(us * 1.1e10), bytes_accessed=int(us * 3.5e7), transcendentals=0),
        )(*args, *([self.last] if skip else []))
        self.last = out[0]
        return out


def exchange(value, orders, step):
    pairs = [(p * 16 + i, p * 16 + j) for p in range(2) for i, j in ROW_PAIRS[orders[p][step]]]
    return lax.ppermute(value, ("dp", "row"), pairs)


def along_col(value, distance):
    return lax.ppermute(value, "col", [(i, (i - distance) % 8) for i in range(8)])


def label_bits(orders):
    index = lax.axis_index("row")
    x, y = index // 4, index % 4
    bits = ((y >> 1) ^ (y & 1), y >> 1, (x >> 1) ^ (x & 1), x >> 1)
    first = lax.axis_index("dp") == 0
    return [jnp.where(first, bits[i], bits[j]) for i, j in zip(*orders)]


def vector(*values):
    return jnp.stack([jnp.asarray(v, jnp.int32) for v in values])


def order_matrix(flip, which, inverse):
    rows = 2 * BLOCK
    shape = (BLOCK, rows) if inverse else (rows, BLOCK)
    local = lax.broadcasted_iota(jnp.int32, shape, 1 if inverse else 0)
    plain = lax.broadcasted_iota(jnp.int32, shape, 0 if inverse else 1)
    wanted = (((local >> 5) ^ flip) << 4) + (local & 15)
    hit = (wanted == plain) & (((local >> 4) & 1) == which)
    return jnp.where(hit, 1.0, 0.0).astype(BF16)


def dot(left, right):
    return jnp.dot(left, right, preferred_element_type=F32)


def dot_cols(left, right):
    return lax.dot_general(left, right, (((1,), (1,)), ((), ())), preferred_element_type=F32)


def dot_rows(left, right):
    return lax.dot_general(left, right, (((0,), (0,)), ((), ())), preferred_element_type=F32)


def tiles(extent):
    return [slice(start, start + TILE) for start in range(0, extent, TILE)]


def near_core(value):
    return pltpu.with_memory_space_constraint(value, pltpu.VMEM)


def pack(line, tokens, cotangent):
    rows, width = tokens.shape

    def kernel(tokens_ref, cotangent_ref, out_ref, first, second):
        copies = [
            pltpu.make_async_copy(tokens_ref, out_ref.at[:, :width], first),
            pltpu.make_async_copy(cotangent_ref, out_ref.at[:, width:], second),
        ]
        for copy in copies:
            copy.start()
        for copy in copies:
            copy.wait()

    return line.call(
        kernel,
        [pltpu.with_memory_space_constraint(x, pltpu.HBM) for x in (tokens, cotangent)],
        [pl.BlockSpec(memory_space=pltpu.HBM)] * 2,
        [pltpu.VMEM((rows, 2 * width), BF16)],
        us=0.1,
        scratch=[pltpu.SemaphoreType.DMA] * 2,
    )[0]


def stage_weights(line, weights):
    def kernel(*refs):
        copies = [pltpu.make_async_copy(refs[k], refs[3 + k], refs[6 + k]) for k in range(3)]
        for copy in copies:
            copy.start()
        for copy in copies:
            copy.wait()

    return line.call(
        kernel,
        [pltpu.with_memory_space_constraint(w, pltpu.HBM) for w in weights],
        [pl.BlockSpec(memory_space=pltpu.HBM)] * 3,
        [pltpu.VMEM(w.shape, w.dtype) for w in weights],
        us=4.5,
        scratch=[pltpu.SemaphoreType.DMA] * 3,
    )


def terms(line, flip, blocks, weights):
    width, hidden = weights[0].shape

    def kernel(flip_ref, first, second, gate_ref, up_ref, down_ref, rows_ref, send, keep):
        rows_ref[...] = (
            dot(order_matrix(flip_ref[0], 0, False), first[...]) + dot(order_matrix(flip_ref[0], 1, False), second[...])
        ).astype(BF16)
        inputs, upstream = rows_ref[:, :width], rows_ref[:, width:]
        for cols in tiles(hidden):
            values = (dot(inputs, gate_ref[:, cols]), dot(inputs, up_ref[:, cols]), dot_cols(upstream, down_ref[cols]))
            for index, value in enumerate(values):
                keep[index, :, cols] = value[:BLOCK]
                send[index, :, cols] = value[BLOCK:].astype(BF16)

    shape = (3, BLOCK, hidden)
    return line.call(
        kernel,
        [flip, *blocks, *map(near_core, weights)],
        [SMEM] + [VMEM] * 5,
        [pltpu.VMEM((2 * BLOCK, 2 * width), BF16), pltpu.VMEM(shape, BF16), pltpu.VMEM(shape, F32)],
        us=3.0,
    )


def add_rows(line, keep, got, kept):
    _, rows, hidden = keep.shape
    half = rows // 2

    def kernel(keep_ref, got_ref, send_ref, next_ref):
        for k in range(3):
            next_ref[k] = (keep_ref[k, :half].astype(F32) + got_ref[k, :half].astype(F32)).astype(kept)
            send_ref[k] = (keep_ref[k, half:].astype(F32) + got_ref[k, half:].astype(F32)).astype(BF16)

    shape = (3, half, hidden)
    return line.call(kernel, [keep, got], [VMEM, VMEM], [pltpu.VMEM(shape, BF16), pltpu.VMEM(shape, kept)], us=rows / 75)


def add_cols(line, bit, keep, got):
    _, rows, hidden = keep.shape
    half = hidden // 2

    def kernel(bit_ref, keep_ref, got_ref, send_ref, next_ref):
        upper = bit_ref[0] == 1
        for k in range(3):
            low = keep_ref[k, :, :half] + got_ref[k, :, :half].astype(F32)
            high = keep_ref[k, :, half:] + got_ref[k, :, half:].astype(F32)
            next_ref[k] = jnp.where(upper, high, low)
            send_ref[k] = jnp.where(upper, low, high)

    shape = (3, rows, half)
    return line.call(kernel, [bit, keep, got], [SMEM, VMEM, VMEM], [pltpu.VMEM(shape, F32), pltpu.VMEM(shape, F32)], us=0.4)


def activate(line, keep, got):
    def kernel(keep_ref, got_ref, out_ref):
        gate, up_val, dhidden = [keep_ref[k] + got_ref[k] for k in range(3)]
        sigma = jax.nn.sigmoid(gate)
        out_ref[0] = (gate * sigma * up_val).astype(BF16)
        out_ref[1] = (dhidden * up_val * sigma * (1.0 + gate * (1.0 - sigma))).astype(BF16)
        out_ref[2] = (dhidden * gate * sigma).astype(BF16)

    return line.call(kernel, [keep, got], [VMEM, VMEM], [pltpu.VMEM(keep.shape, BF16)], us=0.7)[0]


def join_cols(line, bit, near, got):
    _, rows, half = near.shape

    def kernel(bit_ref, near_ref, got_ref, out_ref):
        upper = bit_ref[0] == 1
        for k in range(3):
            out_ref[k, :, :half] = jnp.where(upper, got_ref[k], near_ref[k])
            out_ref[k, :, half:] = jnp.where(upper, near_ref[k], got_ref[k])

    return line.call(kernel, [bit, near, got], [SMEM, VMEM, VMEM], [pltpu.VMEM((3, rows, 2 * half), BF16)], us=0.3)[0]


def join_rows(line, near, got):
    _, rows, hidden = near.shape

    def kernel(near_ref, got_ref, out_ref):
        out_ref[:, :rows] = near_ref[...]
        out_ref[:, rows:] = got_ref[...]

    return line.call(kernel, [near, got], [VMEM, VMEM], [pltpu.VMEM((3, 2 * rows, hidden), BF16)], us=0.8)[0]


def results(line, flip, near, far, weights, us):
    width, hidden = weights[0].shape

    def kernel(flip_ref, near_ref, far_ref, gate_ref, up_ref, down_ref, out0, out1):
        mixed = input_grad = jnp.zeros((2 * BLOCK, width), F32)
        for cols in tiles(hidden):
            parts = [jnp.concatenate([near_ref[k, :, cols], far_ref[k, :, cols]], axis=0) for k in range(3)]
            mixed += dot(parts[0], down_ref[cols])
            input_grad += dot_cols(parts[1], gate_ref[:, cols]) + dot_cols(parts[2], up_ref[:, cols])
        both = jnp.concatenate([mixed, input_grad], axis=1).astype(BF16)
        for j, out in enumerate((out0, out1)):
            out[...] = dot(order_matrix(flip_ref[0], j, True), both).astype(BF16)

    return line.call(
        kernel,
        [flip, near, far, *map(near_core, weights)],
        [SMEM] + [VMEM] * 5,
        [pltpu.VMEM((BLOCK, 2 * width), BF16)] * 2,
        us=us,
    )


def gather_sums(line, total, parts, us):
    def kernel(*refs):
        value = refs[0][...].astype(F32)
        for ref in refs[1:-1]:
            value += ref[...].astype(F32)
        refs[-1][...] = value

    args = ([] if total is None else [total]) + parts
    return line.call(kernel, args, [VMEM] * len(args), [pltpu.VMEM(parts[0].shape, F32)], us=us)[0]


def down_term(line, rows, pieces, held, last):
    width = rows[0].shape[1] // 2
    hidden = pieces[0].shape[2]
    count = len(rows)
    parts = len(pieces)

    def kernel(*refs):
        row_refs, piece_refs, out_ref = refs[:count], refs[count:count + parts], refs[-1]
        upstream = jnp.concatenate([r[:, width:] for r in row_refs], axis=0)
        for cols in tiles(hidden):
            value = dot_rows(jnp.concatenate([p[0, :, cols] for p in piece_refs], axis=0), upstream)
            if held is not None:
                value += refs[count + parts][cols]
            out_ref[cols] = value.astype(out_ref.dtype)

    args = [*rows, *pieces] + ([] if held is None else [held])
    out = pltpu.VMEM((hidden, width), BF16 if last else F32)
    return line.call(kernel, args, [VMEM] * len(args), [out], us=0.02)[0]


def inner_terms(line, rows, pieces, held, last):
    width = rows[0].shape[1] // 2
    hidden = pieces[0].shape[2]
    count = len(rows)
    parts = len(pieces)

    def kernel(*refs):
        row_refs, piece_refs, out_ref = refs[:count], refs[count:count + parts], refs[-1]
        inputs = jnp.concatenate([r[:, :width] for r in row_refs], axis=0).T
        for which in (0, 1):
            for cols in tiles(hidden):
                grads = jnp.concatenate([p[1 + which, :, cols] for p in piece_refs], axis=0)
                value = dot(inputs, grads)
                if held is not None:
                    value += refs[count + parts][which, :, cols]
                out_ref[which, :, cols] = value.astype(out_ref.dtype)

    args = [*rows, *pieces] + ([] if held is None else [held])
    out = pltpu.VMEM((2, width, hidden), BF16 if last else F32)
    return line.call(kernel, args, [VMEM] * len(args), [out], us=0.02)[0]


def stream(line, plan, blocks_at, weights, state):
    owners, *orders = plan
    bits = label_bits(orders)
    flip, last = vector(bits[0] * 4 + bits[1] * 2 + bits[2]), vector(bits[3])
    rows, send, keep = terms(line, flip, [blocks_at[o] for o in owners], weights)
    got = exchange(send, orders, 0)
    yield
    send, keep = add_rows(line, keep, got, F32)
    got = exchange(send, orders, 1)
    yield
    send, keep = add_rows(line, keep, got, F32)
    got = exchange(send, orders, 2)
    yield
    send, keep = add_cols(line, last, keep, got)
    got = exchange(send, orders, 3)
    yield
    near = activate(line, keep, got)
    got = exchange(near, orders, 3)
    yield
    near = join_cols(line, last, near, got)
    got = exchange(near, orders, 2)
    yield
    near = join_rows(line, near, got)
    got = exchange(near, orders, 1)
    yield
    near = join_rows(line, near, got)
    far = exchange(near, orders, 0)
    state["rows"].append(rows)
    state["pieces"] += [near, far]
    yield
    parts = results(line, flip, near, far, weights, 1.0 if owners == STREAMS[1][0] else 0.3)
    parts = [along_col(part, -owner) if owner else part for owner, part in zip(owners, parts)]
    state["parts"].append(parts)


def on_device(tokens, cotangent, *weights):
    width = tokens.shape[1]
    line = Line()
    blocks_at = {0: pack(line, tokens, cotangent)}
    for distance in (1, 2, 3, 4):
        blocks_at[distance] = along_col(blocks_at[distance - 1], 1)
        if distance < 4:
            blocks_at[-distance] = along_col(blocks_at[1 - distance], -1)

    weights = stage_weights(line, weights)
    state = {"rows": [], "pieces": [], "parts": []}
    streams = [stream(line, plan, blocks_at, weights, state) for plan in STREAMS]
    grads, held, total = {}, {}, None
    for name in ORDER:
        if name in "xyz":
            count = "xyz".index(name) + 1
            waiting = sum(state["parts"][:count], [])
            del state["parts"][:count]
            total = gather_sums(line, total, waiting, 0.3 if name == "x" else 10.0)
            continue
        if name in "pq":
            make = inner_terms if name == "p" else down_term
            held[name] = make(line, state["rows"][:3], state["pieces"][:6], None, False)
        elif name in "id":
            make, first = (inner_terms, "p") if name == "i" else (down_term, "q")
            mine = make(line, state["rows"][3:], state["pieces"][6:], held[first], True)
            grads[name] = (mine, lax.ppermute(mine, "dp", [(0, 1), (1, 0)]))
        else:
            next(streams[int(name)], None)

    def both(left, right):
        return (left.astype(F32) + right.astype(F32)).astype(BF16)

    mine, other = grads["i"]
    return (
        total[:, :width].astype(BF16),
        total[:, width:].astype(BF16),
        both(mine[0], other[0]),
        both(mine[1], other[1]),
        both(*grads["d"]),
    )


def solution(mesh):
    specs = (
        P(("dp", "col"), "row"),
        P(("dp", "col"), "row"),
        P("row", "col"),
        P("row", "col"),
        P("col", "row"),
    )
    return jax.shard_map(on_device, mesh=mesh, in_specs=specs, out_specs=specs, check_vma=False)
```

```python
import jax
import jax.numpy as jnp
from jax import lax
from jax.experimental import pallas as pl
from jax.experimental.pallas import tpu as pltpu
from jax.sharding import PartitionSpec as P

F32 = jnp.float32
BF16 = jnp.bfloat16

ROW_PAIRS = (
    [(i, (i // 4) * 4 + ((i % 4) ^ 1)) for i in range(16)],
    [(i, (i // 4) * 4 + (3 - i % 4)) for i in range(16)],
    [(i, ((i // 4) ^ 1) * 4 + i % 4) for i in range(16)],
    [(i, (3 - i // 4) * 4 + i % 4) for i in range(16)],
)

STREAMS = (
    ((1, -1), (1, 2, 0, 3), (0, 3, 1, 2)),
    ((2, -2), (2, 0, 3, 1), (3, 1, 2, 0)),
    ((3, -3), (0, 3, 2, 1), (1, 2, 3, 0)),
    ((0, 4), (0, 2, 3, 1), (1, 3, 2, 0)),
)

ORDER = "0123010210321032103210321302312031x2pq3xidy"

BLOCK = 128
TILE = 256
GROUP = 16
VMEM = pl.BlockSpec(memory_space=pltpu.VMEM)
SMEM = pl.BlockSpec(memory_space=pltpu.SMEM)
ANY = pl.BlockSpec(memory_space=pl.ANY)


class Line:
    def __init__(self):
        self.last = None

    def call(self, kernel, args, in_specs, out_shape, us, scratch=(), vmem=6):
        inputs = len(args)
        skip = 0 if self.last is None else 1

        def body(*refs):
            kernel(*refs[:inputs], *refs[inputs + skip:])

        out = pl.pallas_call(
            body,
            in_specs=list(in_specs) + [ANY] * skip,
            out_specs=[VMEM] * len(out_shape),
            out_shape=out_shape,
            scratch_shapes=scratch,
            compiler_params=pltpu.CompilerParams(vmem_limit_bytes=vmem << 20),
            cost_estimate=pl.CostEstimate(flops=int(us * 1.1e10), bytes_accessed=int(us * 3.5e7), transcendentals=0),
        )(*args, *([self.last] if skip else []))
        self.last = out[0]
        return out


def exchange(value, orders, step):
    pairs = [(p * 16 + i, p * 16 + j) for p in range(2) for i, j in ROW_PAIRS[orders[p][step]]]
    return lax.ppermute(value, ("dp", "row"), pairs)


def along_col(value, distance):
    return lax.ppermute(value, "col", [(i, (i - distance) % 8) for i in range(8)])


def label_bits(orders):
    index = lax.axis_index("row")
    x, y = index // 4, index % 4
    bits = ((y >> 1) ^ (y & 1), y >> 1, (x >> 1) ^ (x & 1), x >> 1)
    first = lax.axis_index("dp") == 0
    return [jnp.where(first, bits[i], bits[j]) for i, j in zip(*orders)]


def vector(*values):
    return jnp.stack([jnp.asarray(v, jnp.int32) for v in values])


def order_matrix(flip, which, inverse):
    rows = 2 * BLOCK
    shape = (BLOCK, rows) if inverse else (rows, BLOCK)
    local = lax.broadcasted_iota(jnp.int32, shape, 1 if inverse else 0)
    plain = lax.broadcasted_iota(jnp.int32, shape, 0 if inverse else 1)
    wanted = (((local >> 5) ^ flip) << 4) + (local & 15)
    hit = (wanted == plain) & (((local >> 4) & 1) == which)
    return jnp.where(hit, 1.0, 0.0).astype(BF16)


def dot(left, right):
    return jnp.dot(left, right, preferred_element_type=F32)


def dot_cols(left, right):
    return lax.dot_general(left, right, (((1,), (1,)), ((), ())), preferred_element_type=F32)


def dot_rows(left, right):
    return lax.dot_general(left, right, (((0,), (0,)), ((), ())), preferred_element_type=F32)


def tiles(extent):
    return [slice(start, start + TILE) for start in range(0, extent, TILE)]


def near_core(value):
    return pltpu.with_memory_space_constraint(value, pltpu.VMEM)


def pack(line, tokens, cotangent):
    rows, width = tokens.shape

    def kernel(tokens_ref, cotangent_ref, out_ref, first, second):
        copies = [
            pltpu.make_async_copy(tokens_ref, out_ref.at[:, :width], first),
            pltpu.make_async_copy(cotangent_ref, out_ref.at[:, width:], second),
        ]
        for copy in copies:
            copy.start()
        for copy in copies:
            copy.wait()

    return line.call(
        kernel,
        [pltpu.with_memory_space_constraint(x, pltpu.HBM) for x in (tokens, cotangent)],
        [pl.BlockSpec(memory_space=pltpu.HBM)] * 2,
        [pltpu.VMEM((rows, 2 * width), BF16)],
        us=0.1,
        scratch=[pltpu.SemaphoreType.DMA] * 2,
    )[0]


def stage_weights(line, weights):
    def kernel(*refs):
        copies = [pltpu.make_async_copy(refs[k], refs[3 + k], refs[6 + k]) for k in range(3)]
        for copy in copies:
            copy.start()
        for copy in copies:
            copy.wait()

    return line.call(
        kernel,
        [pltpu.with_memory_space_constraint(w, pltpu.HBM) for w in weights],
        [pl.BlockSpec(memory_space=pltpu.HBM)] * 3,
        [pltpu.VMEM(w.shape, w.dtype) for w in weights],
        us=4.5,
        scratch=[pltpu.SemaphoreType.DMA] * 3,
    )


def terms(line, flip, blocks, weights):
    width, hidden = weights[0].shape

    def kernel(flip_ref, first, second, gate_ref, up_ref, down_ref, rows_ref, send, keep):
        rows_ref[...] = (
            dot(order_matrix(flip_ref[0], 0, False), first[...]) + dot(order_matrix(flip_ref[0], 1, False), second[...])
        ).astype(BF16)
        inputs, upstream = rows_ref[:, :width], rows_ref[:, width:]
        for cols in tiles(hidden):
            values = (dot(inputs, gate_ref[:, cols]), dot(inputs, up_ref[:, cols]), dot_cols(upstream, down_ref[cols]))
            for index, value in enumerate(values):
                keep[index, :, cols] = value[:BLOCK]
                send[index, :, cols] = value[BLOCK:].astype(BF16)

    shape = (3, BLOCK, hidden)
    return line.call(
        kernel,
        [flip, *blocks, *map(near_core, weights)],
        [SMEM] + [VMEM] * 5,
        [pltpu.VMEM((2 * BLOCK, 2 * width), BF16), pltpu.VMEM(shape, BF16), pltpu.VMEM(shape, F32)],
        us=3.0,
    )


def add_rows(line, keep, got, kept):
    _, rows, hidden = keep.shape
    half = rows // 2

    def kernel(keep_ref, got_ref, send_ref, next_ref):
        for k in range(3):
            next_ref[k] = (keep_ref[k, :half].astype(F32) + got_ref[k, :half].astype(F32)).astype(kept)
            send_ref[k] = (keep_ref[k, half:].astype(F32) + got_ref[k, half:].astype(F32)).astype(BF16)

    shape = (3, half, hidden)
    return line.call(kernel, [keep, got], [VMEM, VMEM], [pltpu.VMEM(shape, BF16), pltpu.VMEM(shape, kept)], us=rows / 75)


def add_cols(line, bit, keep, got):
    _, rows, hidden = keep.shape
    half = hidden // 2

    def kernel(bit_ref, keep_ref, got_ref, send_ref, next_ref):
        upper = bit_ref[0] == 1
        for k in range(3):
            low = keep_ref[k, :, :half] + got_ref[k, :, :half].astype(F32)
            high = keep_ref[k, :, half:] + got_ref[k, :, half:].astype(F32)
            next_ref[k] = jnp.where(upper, high, low)
            send_ref[k] = jnp.where(upper, low, high)

    shape = (3, rows, half)
    return line.call(kernel, [bit, keep, got], [SMEM, VMEM, VMEM], [pltpu.VMEM(shape, F32), pltpu.VMEM(shape, F32)], us=0.4)


def activate(line, keep, got):
    def kernel(keep_ref, got_ref, out_ref):
        gate, up_val, dhidden = [keep_ref[k] + got_ref[k] for k in range(3)]
        sigma = jax.nn.sigmoid(gate)
        out_ref[0] = (gate * sigma * up_val).astype(BF16)
        out_ref[1] = (dhidden * up_val * sigma * (1.0 + gate * (1.0 - sigma))).astype(BF16)
        out_ref[2] = (dhidden * gate * sigma).astype(BF16)

    return line.call(kernel, [keep, got], [VMEM, VMEM], [pltpu.VMEM(keep.shape, BF16)], us=0.7)[0]


def join_cols(line, bit, near, got):
    _, rows, half = near.shape

    def kernel(bit_ref, near_ref, got_ref, out_ref):
        upper = bit_ref[0] == 1
        for k in range(3):
            out_ref[k, :, :half] = jnp.where(upper, got_ref[k], near_ref[k])
            out_ref[k, :, half:] = jnp.where(upper, near_ref[k], got_ref[k])

    return line.call(kernel, [bit, near, got], [SMEM, VMEM, VMEM], [pltpu.VMEM((3, rows, 2 * half), BF16)], us=0.3)[0]


def join_rows(line, near, got):
    _, rows, hidden = near.shape

    def kernel(near_ref, got_ref, out_ref):
        out_ref[:, :rows] = near_ref[...]
        out_ref[:, rows:] = got_ref[...]

    return line.call(kernel, [near, got], [VMEM, VMEM], [pltpu.VMEM((3, 2 * rows, hidden), BF16)], us=0.8)[0]


def results(line, flip, near, far, weights, us):
    width, hidden = weights[0].shape

    def kernel(flip_ref, near_ref, far_ref, gate_ref, up_ref, down_ref, out0, out1):
        mixed = input_grad = jnp.zeros((2 * BLOCK, width), F32)
        for cols in tiles(hidden):
            parts = [jnp.concatenate([near_ref[k, :, cols], far_ref[k, :, cols]], axis=0) for k in range(3)]
            mixed += dot(parts[0], down_ref[cols])
            input_grad += dot_cols(parts[1], gate_ref[:, cols]) + dot_cols(parts[2], up_ref[:, cols])
        both = jnp.concatenate([mixed, input_grad], axis=1).astype(BF16)
        for j, out in enumerate((out0, out1)):
            out[...] = dot(order_matrix(flip_ref[0], j, True), both).astype(BF16)

    return line.call(
        kernel,
        [flip, near, far, *map(near_core, weights)],
        [SMEM] + [VMEM] * 5,
        [pltpu.VMEM((BLOCK, 2 * width), BF16)] * 2,
        us=us,
    )


def gather_sums(line, total, parts, us):
    def kernel(*refs):
        value = refs[0][...].astype(F32)
        for ref in refs[1:-1]:
            value += ref[...].astype(F32)
        refs[-1][...] = value

    args = ([] if total is None else [total]) + parts
    return line.call(kernel, args, [VMEM] * len(args), [pltpu.VMEM(parts[0].shape, F32)], us=us)[0]


def down_term(line, rows, pieces, held, last):
    width = rows[0].shape[1] // 2
    hidden = pieces[0].shape[2]
    count = len(rows)
    parts = len(pieces)

    def kernel(*refs):
        row_refs, piece_refs, out_ref = refs[:count], refs[count:count + parts], refs[-1]
        upstream = jnp.concatenate([r[:, width:] for r in row_refs], axis=0)
        for cols in tiles(hidden):
            value = dot_rows(jnp.concatenate([p[0, :, cols] for p in piece_refs], axis=0), upstream)
            if held is not None:
                value += refs[count + parts][cols]
            out_ref[cols] = value.astype(out_ref.dtype)

    args = [*rows, *pieces] + ([] if held is None else [held])
    out = pltpu.VMEM((hidden, width), BF16 if last else F32)
    return line.call(kernel, args, [VMEM] * len(args), [out], us=0.02)[0]


def inner_terms(line, rows, pieces, held, last):
    width = rows[0].shape[1] // 2
    hidden = pieces[0].shape[2]
    count = len(rows)
    parts = len(pieces)

    def kernel(*refs):
        row_refs, piece_refs, out_ref = refs[:count], refs[count:count + parts], refs[-1]
        inputs = jnp.concatenate([r[:, :width] for r in row_refs], axis=0).T
        for which in (0, 1):
            for cols in tiles(hidden):
                grads = jnp.concatenate([p[1 + which, :, cols] for p in piece_refs], axis=0)
                value = dot(inputs, grads)
                if held is not None:
                    value += refs[count + parts][which, :, cols]
                out_ref[which, :, cols] = value.astype(out_ref.dtype)

    args = [*rows, *pieces] + ([] if held is None else [held])
    out = pltpu.VMEM((2, width, hidden), BF16 if last else F32)
    return line.call(kernel, args, [VMEM] * len(args), [out], us=0.02)[0]


def stream(line, plan, blocks_at, weights, state):
    owners, *orders = plan
    bits = label_bits(orders)
    flip, last = vector(bits[0] * 4 + bits[1] * 2 + bits[2]), vector(bits[3])
    rows, send, keep = terms(line, flip, [blocks_at[o] for o in owners], weights)
    got = exchange(send, orders, 0)
    yield
    send, keep = add_rows(line, keep, got, F32)
    got = exchange(send, orders, 1)
    yield
    send, keep = add_rows(line, keep, got, F32)
    got = exchange(send, orders, 2)
    yield
    send, keep = add_cols(line, last, keep, got)
    got = exchange(send, orders, 3)
    yield
    near = activate(line, keep, got)
    got = exchange(near, orders, 3)
    yield
    near = join_cols(line, last, near, got)
    got = exchange(near, orders, 2)
    yield
    near = join_rows(line, near, got)
    got = exchange(near, orders, 1)
    yield
    near = join_rows(line, near, got)
    far = exchange(near, orders, 0)
    state["rows"].append(rows)
    state["pieces"] += [near, far]
    yield
    parts = results(line, flip, near, far, weights, 1.0 if owners == STREAMS[1][0] else 0.3)
    parts = [along_col(part, -owner) if owner else part for owner, part in zip(owners, parts)]
    state["parts"].append(parts)


def on_device(tokens, cotangent, *weights):
    width = tokens.shape[1]
    line = Line()
    blocks_at = {0: pack(line, tokens, cotangent)}
    for distance in (1, 2, 3, 4):
        blocks_at[distance] = along_col(blocks_at[distance - 1], 1)
        if distance < 4:
            blocks_at[-distance] = along_col(blocks_at[1 - distance], -1)

    weights = stage_weights(line, weights)
    state = {"rows": [], "pieces": [], "parts": []}
    streams = [stream(line, plan, blocks_at, weights, state) for plan in STREAMS]
    grads, held, total = {}, {}, None
    for name in ORDER:
        if name in "xyz":
            count = "xyz".index(name) + 1
            waiting = sum(state["parts"][:count], [])
            del state["parts"][:count]
            total = gather_sums(line, total, waiting, 0.3 if name == "x" else 10.0)
            continue
        if name in "pq":
            make = inner_terms if name == "p" else down_term
            held[name] = make(line, state["rows"][:3], state["pieces"][:6], None, False)
        elif name in "id":
            make, first = (inner_terms, "p") if name == "i" else (down_term, "q")
            mine = make(line, state["rows"][3:], state["pieces"][6:], held[first], True)
            grads[name] = (mine, lax.ppermute(mine, "dp", [(0, 1), (1, 0)]))
        else:
            next(streams[int(name)], None)

    def both(left, right):
        return (left.astype(F32) + right.astype(F32)).astype(BF16)

    mine, other = grads["i"]
    return (
        total[:, :width].astype(BF16),
        total[:, width:].astype(BF16),
        both(mine[0], other[0]),
        both(mine[1], other[1]),
        both(*grads["d"]),
    )


def solution(mesh):
    specs = (
        P(("dp", "col"), "row"),
        P(("dp", "col"), "row"),
        P("row", "col"),
        P("row", "col"),
        P("col", "row"),
    )
    return jax.shard_map(on_device, mesh=mesh, in_specs=specs, out_specs=specs, check_vma=False)
```

```python
import jax
import jax.numpy as jnp
from jax import lax
from jax.experimental import pallas as pl
from jax.experimental.pallas import tpu as pltpu
from jax.sharding import PartitionSpec as P

F32 = jnp.float32
BF16 = jnp.bfloat16

ROW_PAIRS = (
    [(i, (i // 4) * 4 + ((i % 4) ^ 1)) for i in range(16)],
    [(i, (i // 4) * 4 + (3 - i % 4)) for i in range(16)],
    [(i, ((i // 4) ^ 1) * 4 + i % 4) for i in range(16)],
    [(i, (3 - i // 4) * 4 + i % 4) for i in range(16)],
)

STREAMS = (
    ((1, -1), (1, 2, 0, 3), (0, 3, 1, 2)),
    ((2, -2), (2, 0, 3, 1), (3, 1, 2, 0)),
    ((3, -3), (2, 0, 3, 1), (3, 1, 2, 0)),
    ((0, 4), (0, 2, 3, 1), (1, 3, 2, 0)),
)

ORDER = "0123010210321032103210321302312031x2pq3xidy"

BLOCK = 128
TILE = 256
GROUP = 16
VMEM = pl.BlockSpec(memory_space=pltpu.VMEM)
SMEM = pl.BlockSpec(memory_space=pltpu.SMEM)
ANY = pl.BlockSpec(memory_space=pl.ANY)


class Line:
    def __init__(self):
        self.last = None

    def call(self, kernel, args, in_specs, out_shape, us, scratch=(), vmem=6):
        inputs = len(args)
        skip = 0 if self.last is None else 1

        def body(*refs):
            kernel(*refs[:inputs], *refs[inputs + skip:])

        out = pl.pallas_call(
            body,
            in_specs=list(in_specs) + [ANY] * skip,
            out_specs=[VMEM] * len(out_shape),
            out_shape=out_shape,
            scratch_shapes=scratch,
            compiler_params=pltpu.CompilerParams(vmem_limit_bytes=vmem << 20),
            cost_estimate=pl.CostEstimate(flops=int(us * 1.1e10), bytes_accessed=int(us * 3.5e7), transcendentals=0),
        )(*args, *([self.last] if skip else []))
        self.last = out[0]
        return out


def exchange(value, orders, step):
    pairs = [(p * 16 + i, p * 16 + j) for p in range(2) for i, j in ROW_PAIRS[orders[p][step]]]
    return lax.ppermute(value, ("dp", "row"), pairs)


def along_col(value, distance):
    return lax.ppermute(value, "col", [(i, (i - distance) % 8) for i in range(8)])


def label_bits(orders):
    index = lax.axis_index("row")
    x, y = index // 4, index % 4
    bits = ((y >> 1) ^ (y & 1), y >> 1, (x >> 1) ^ (x & 1), x >> 1)
    first = lax.axis_index("dp") == 0
    return [jnp.where(first, bits[i], bits[j]) for i, j in zip(*orders)]


def vector(*values):
    return jnp.stack([jnp.asarray(v, jnp.int32) for v in values])


def order_matrix(flip, which, inverse):
    rows = 2 * BLOCK
    shape = (BLOCK, rows) if inverse else (rows, BLOCK)
    local = lax.broadcasted_iota(jnp.int32, shape, 1 if inverse else 0)
    plain = lax.broadcasted_iota(jnp.int32, shape, 0 if inverse else 1)
    wanted = (((local >> 5) ^ flip) << 4) + (local & 15)
    hit = (wanted == plain) & (((local >> 4) & 1) == which)
    return jnp.where(hit, 1.0, 0.0).astype(BF16)


def dot(left, right):
    return jnp.dot(left, right, preferred_element_type=F32)


def dot_cols(left, right):
    return lax.dot_general(left, right, (((1,), (1,)), ((), ())), preferred_element_type=F32)


def dot_rows(left, right):
    return lax.dot_general(left, right, (((0,), (0,)), ((), ())), preferred_element_type=F32)


def tiles(extent):
    return [slice(start, start + TILE) for start in range(0, extent, TILE)]


def near_core(value):
    return pltpu.with_memory_space_constraint(value, pltpu.VMEM)


def pack(line, tokens, cotangent):
    rows, width = tokens.shape

    def kernel(tokens_ref, cotangent_ref, out_ref, first, second):
        copies = [
            pltpu.make_async_copy(tokens_ref, out_ref.at[:, :width], first),
            pltpu.make_async_copy(cotangent_ref, out_ref.at[:, width:], second),
        ]
        for copy in copies:
            copy.start()
        for copy in copies:
            copy.wait()

    return line.call(
        kernel,
        [pltpu.with_memory_space_constraint(x, pltpu.HBM) for x in (tokens, cotangent)],
        [pl.BlockSpec(memory_space=pltpu.HBM)] * 2,
        [pltpu.VMEM((rows, 2 * width), BF16)],
        us=0.1,
        scratch=[pltpu.SemaphoreType.DMA] * 2,
    )[0]


def stage_weights(line, weights):
    def kernel(*refs):
        copies = [pltpu.make_async_copy(refs[k], refs[3 + k], refs[6 + k]) for k in range(3)]
        for copy in copies:
            copy.start()
        for copy in copies:
            copy.wait()

    return line.call(
        kernel,
        [pltpu.with_memory_space_constraint(w, pltpu.HBM) for w in weights],
        [pl.BlockSpec(memory_space=pltpu.HBM)] * 3,
        [pltpu.VMEM(w.shape, w.dtype) for w in weights],
        us=4.5,
        scratch=[pltpu.SemaphoreType.DMA] * 3,
    )


def terms(line, flip, blocks, weights):
    width, hidden = weights[0].shape

    def kernel(flip_ref, first, second, gate_ref, up_ref, down_ref, rows_ref, send, keep):
        rows_ref[...] = (
            dot(order_matrix(flip_ref[0], 0, False), first[...]) + dot(order_matrix(flip_ref[0], 1, False), second[...])
        ).astype(BF16)
        inputs, upstream = rows_ref[:, :width], rows_ref[:, width:]
        for cols in tiles(hidden):
            values = (dot(inputs, gate_ref[:, cols]), dot(inputs, up_ref[:, cols]), dot_cols(upstream, down_ref[cols]))
            for index, value in enumerate(values):
                keep[index, :, cols] = value[:BLOCK]
                send[index, :, cols] = value[BLOCK:].astype(BF16)

    shape = (3, BLOCK, hidden)
    return line.call(
        kernel,
        [flip, *blocks, *map(near_core, weights)],
        [SMEM] + [VMEM] * 5,
        [pltpu.VMEM((2 * BLOCK, 2 * width), BF16), pltpu.VMEM(shape, BF16), pltpu.VMEM(shape, F32)],
        us=3.0,
    )


def add_rows(line, keep, got, kept):
    _, rows, hidden = keep.shape
    half = rows // 2

    def kernel(keep_ref, got_ref, send_ref, next_ref):
        for k in range(3):
            next_ref[k] = (keep_ref[k, :half].astype(F32) + got_ref[k, :half].astype(F32)).astype(kept)
            send_ref[k] = (keep_ref[k, half:].astype(F32) + got_ref[k, half:].astype(F32)).astype(BF16)

    shape = (3, half, hidden)
    return line.call(kernel, [keep, got], [VMEM, VMEM], [pltpu.VMEM(shape, BF16), pltpu.VMEM(shape, kept)], us=rows / 75)


def add_cols(line, bit, keep, got):
    _, rows, hidden = keep.shape
    half = hidden // 2

    def kernel(bit_ref, keep_ref, got_ref, send_ref, next_ref):
        upper = bit_ref[0] == 1
        for k in range(3):
            low = keep_ref[k, :, :half] + got_ref[k, :, :half].astype(F32)
            high = keep_ref[k, :, half:] + got_ref[k, :, half:].astype(F32)
            next_ref[k] = jnp.where(upper, high, low)
            send_ref[k] = jnp.where(upper, low, high)

    shape = (3, rows, half)
    return line.call(kernel, [bit, keep, got], [SMEM, VMEM, VMEM], [pltpu.VMEM(shape, F32), pltpu.VMEM(shape, F32)], us=0.4)


def activate(line, keep, got):
    def kernel(keep_ref, got_ref, out_ref):
        gate, up_val, dhidden = [keep_ref[k] + got_ref[k] for k in range(3)]
        sigma = jax.nn.sigmoid(gate)
        out_ref[0] = (gate * sigma * up_val).astype(BF16)
        out_ref[1] = (dhidden * up_val * sigma * (1.0 + gate * (1.0 - sigma))).astype(BF16)
        out_ref[2] = (dhidden * gate * sigma).astype(BF16)

    return line.call(kernel, [keep, got], [VMEM, VMEM], [pltpu.VMEM(keep.shape, BF16)], us=0.7)[0]


def join_cols(line, bit, near, got):
    _, rows, half = near.shape

    def kernel(bit_ref, near_ref, got_ref, out_ref):
        upper = bit_ref[0] == 1
        for k in range(3):
            out_ref[k, :, :half] = jnp.where(upper, got_ref[k], near_ref[k])
            out_ref[k, :, half:] = jnp.where(upper, near_ref[k], got_ref[k])

    return line.call(kernel, [bit, near, got], [SMEM, VMEM, VMEM], [pltpu.VMEM((3, rows, 2 * half), BF16)], us=0.3)[0]


def join_rows(line, near, got):
    _, rows, hidden = near.shape

    def kernel(near_ref, got_ref, out_ref):
        out_ref[:, :rows] = near_ref[...]
        out_ref[:, rows:] = got_ref[...]

    return line.call(kernel, [near, got], [VMEM, VMEM], [pltpu.VMEM((3, 2 * rows, hidden), BF16)], us=0.8)[0]


def results(line, flip, near, far, weights, us):
    width, hidden = weights[0].shape

    def kernel(flip_ref, near_ref, far_ref, gate_ref, up_ref, down_ref, out0, out1):
        mixed = input_grad = jnp.zeros((2 * BLOCK, width), F32)
        for cols in tiles(hidden):
            parts = [jnp.concatenate([near_ref[k, :, cols], far_ref[k, :, cols]], axis=0) for k in range(3)]
            mixed += dot(parts[0], down_ref[cols])
            input_grad += dot_cols(parts[1], gate_ref[:, cols]) + dot_cols(parts[2], up_ref[:, cols])
        both = jnp.concatenate([mixed, input_grad], axis=1).astype(BF16)
        for j, out in enumerate((out0, out1)):
            out[...] = dot(order_matrix(flip_ref[0], j, True), both).astype(BF16)

    return line.call(
        kernel,
        [flip, near, far, *map(near_core, weights)],
        [SMEM] + [VMEM] * 5,
        [pltpu.VMEM((BLOCK, 2 * width), BF16)] * 2,
        us=us,
    )


def gather_sums(line, total, parts, us):
    def kernel(*refs):
        value = refs[0][...].astype(F32)
        for ref in refs[1:-1]:
            value += ref[...].astype(F32)
        refs[-1][...] = value

    args = ([] if total is None else [total]) + parts
    return line.call(kernel, args, [VMEM] * len(args), [pltpu.VMEM(parts[0].shape, F32)], us=us)[0]


def down_term(line, rows, pieces, held, last):
    width = rows[0].shape[1] // 2
    hidden = pieces[0].shape[2]
    count = len(rows)
    parts = len(pieces)

    def kernel(*refs):
        row_refs, piece_refs, out_ref = refs[:count], refs[count:count + parts], refs[-1]
        upstream = jnp.concatenate([r[:, width:] for r in row_refs], axis=0)
        for cols in tiles(hidden):
            value = dot_rows(jnp.concatenate([p[0, :, cols] for p in piece_refs], axis=0), upstream)
            if held is not None:
                value += refs[count + parts][cols]
            out_ref[cols] = value.astype(out_ref.dtype)

    args = [*rows, *pieces] + ([] if held is None else [held])
    out = pltpu.VMEM((hidden, width), BF16 if last else F32)
    return line.call(kernel, args, [VMEM] * len(args), [out], us=0.02)[0]


def inner_terms(line, rows, pieces, held, last):
    width = rows[0].shape[1] // 2
    hidden = pieces[0].shape[2]
    count = len(rows)
    parts = len(pieces)

    def kernel(*refs):
        row_refs, piece_refs, out_ref = refs[:count], refs[count:count + parts], refs[-1]
        inputs = jnp.concatenate([r[:, :width] for r in row_refs], axis=0).T
        for which in (0, 1):
            for cols in tiles(hidden):
                grads = jnp.concatenate([p[1 + which, :, cols] for p in piece_refs], axis=0)
                value = dot(inputs, grads)
                if held is not None:
                    value += refs[count + parts][which, :, cols]
                out_ref[which, :, cols] = value.astype(out_ref.dtype)

    args = [*rows, *pieces] + ([] if held is None else [held])
    out = pltpu.VMEM((2, width, hidden), BF16 if last else F32)
    return line.call(kernel, args, [VMEM] * len(args), [out], us=0.02)[0]


def stream(line, plan, blocks_at, weights, state):
    owners, *orders = plan
    bits = label_bits(orders)
    flip, last = vector(bits[0] * 4 + bits[1] * 2 + bits[2]), vector(bits[3])
    rows, send, keep = terms(line, flip, [blocks_at[o] for o in owners], weights)
    got = exchange(send, orders, 0)
    yield
    send, keep = add_rows(line, keep, got, F32)
    got = exchange(send, orders, 1)
    yield
    send, keep = add_rows(line, keep, got, F32)
    got = exchange(send, orders, 2)
    yield
    send, keep = add_cols(line, last, keep, got)
    got = exchange(send, orders, 3)
    yield
    near = activate(line, keep, got)
    got = exchange(near, orders, 3)
    yield
    near = join_cols(line, last, near, got)
    got = exchange(near, orders, 2)
    yield
    near = join_rows(line, near, got)
    got = exchange(near, orders, 1)
    yield
    near = join_rows(line, near, got)
    far = exchange(near, orders, 0)
    state["rows"].append(rows)
    state["pieces"] += [near, far]
    yield
    parts = results(line, flip, near, far, weights, 1.0 if owners == STREAMS[1][0] else 0.3)
    parts = [along_col(part, -owner) if owner else part for owner, part in zip(owners, parts)]
    state["parts"].append(parts)


def on_device(tokens, cotangent, *weights):
    width = tokens.shape[1]
    line = Line()
    blocks_at = {0: pack(line, tokens, cotangent)}
    for distance in (1, 2, 3, 4):
        blocks_at[distance] = along_col(blocks_at[distance - 1], 1)
        if distance < 4:
            blocks_at[-distance] = along_col(blocks_at[1 - distance], -1)

    weights = stage_weights(line, weights)
    state = {"rows": [], "pieces": [], "parts": []}
    streams = [stream(line, plan, blocks_at, weights, state) for plan in STREAMS]
    grads, held, total = {}, {}, None
    for name in ORDER:
        if name in "xyz":
            count = "xyz".index(name) + 1
            waiting = sum(state["parts"][:count], [])
            del state["parts"][:count]
            total = gather_sums(line, total, waiting, 0.3 if name == "x" else 10.0)
            continue
        if name in "pq":
            make = inner_terms if name == "p" else down_term
            held[name] = make(line, state["rows"][:3], state["pieces"][:6], None, False)
        elif name in "id":
            make, first = (inner_terms, "p") if name == "i" else (down_term, "q")
            mine = make(line, state["rows"][3:], state["pieces"][6:], held[first], True)
            grads[name] = (mine, lax.ppermute(mine, "dp", [(0, 1), (1, 0)]))
        else:
            next(streams[int(name)], None)

    def both(left, right):
        return (left.astype(F32) + right.astype(F32)).astype(BF16)

    mine, other = grads["i"]
    return (
        total[:, :width].astype(BF16),
        total[:, width:].astype(BF16),
        both(mine[0], other[0]),
        both(mine[1], other[1]),
        both(*grads["d"]),
    )


def solution(mesh):
    specs = (
        P(("dp", "col"), "row"),
        P(("dp", "col"), "row"),
        P("row", "col"),
        P("row", "col"),
        P("col", "row"),
    )
    return jax.shard_map(on_device, mesh=mesh, in_specs=specs, out_specs=specs, check_vma=False)
```
